32 devices in a mesh: dom: 8 (over z, x), face: 4 (over y, core).
Axes of the slice: x: 2, y: 2, z: 4, core: 2. Of those that a mesh axis runs over, the one named last changes fastest.
Arguments:
- elem_state: bfloat16 [256, 320], P(('dom', 'face')), may hold values from -6 to 6
- face_metric: bfloat16 [1024, 320], P(('dom', 'face')), may hold values from 0.5 to 2
- right_side: float32 [256, 320], P(('dom', 'face'))
- block_inverse: bfloat16 [256, 320, 320], P(('dom', 'face')), as said below
- trace_basis: bfloat16 [320, 320], replicated, may hold values from -0.3125 to 0.3125
- flux_basis: bfloat16 [320, 320], replicated, may hold values from -0.3125 to 0.3125
- face_rows: int32 [1024], P(('dom', 'face')), may hold values from 0 to 7
- face_cols: int32 [1024], P(('dom', 'face')), may hold values from 0 to 31
- face_counts: int32 [32], P(('dom', 'face')), may hold values from 1 to 32, as said below
Outputs:
- solution: float32 [256, 320], P(('dom', 'face'))
- residual: float32 [256, 320], P(('dom', 'face'))
The draws below stay inside these ranges and needn't reach their ends.
Inputs may be any that keep to these rules, and one draw needn't show every extreme that they name: The first face_counts[p] slots of device p are live, the others are not; some device has all 32 slots live. `block_inverse`: each block is a diagonal part with entries between 0.5 and 1 plus a dense part whose entries, those on the diagonal included, are of order 320 ** -0.5 or smaller.
All inputs are finite; a program needn't handle non-finite values.
Results may differ from the reference program's by a relative error of at most 0.0044.
Values may be sent and summed in bfloat16 or wider, within the bound.
A program may use at most 64 MiB of HBM per device.

```python
import math
import jax
import jax.numpy as jnp
from jax import lax

NV = 320
E_DEV = 8
F_DEV = 32
E_GRP = 32
ELEMS = 256
FACES = 1024
N_DOM = 8
N_FACE = 4


def draw_block_inverse(key, part):
    key_diag, key_off = jax.random.split(key)
    diag_vals = jax.random.uniform(key_diag, (ELEMS, NV), jnp.float32, 0.5, 1.0)
    off_diag = jax.random.normal(key_off, (ELEMS, NV, NV), jnp.float32) * (0.5 / math.sqrt(NV))
    return (off_diag + diag_vals[:, :, None] * jnp.eye(NV, dtype=jnp.float32)[None, :, :]).astype(jnp.bfloat16)


def draw_right_side(key, part):
    key_vals = jax.random.fold_in(key, 0)
    rise = 1.0 + 2.0 * jnp.arange(ELEMS, dtype=jnp.float32) / max(ELEMS - 1, 1)
    values = jax.random.normal(key_vals, (ELEMS, NV), jnp.float32)
    return values * rise[:, None]


def draw_face_counts(key, part):
    total = FACES // F_DEV
    key_a, key_b = jax.random.split(key)
    drawn = jax.random.randint(key_a, (total,), max(1, F_DEV // 4), F_DEV + 1)
    chosen = jax.random.randint(key_b, (), 0, total)
    return jnp.where(jnp.arange(total) == chosen, F_DEV, drawn).astype(jnp.int32)


def place_ends(array, rng, low, high):
    dims = array.shape
    place = [jax.random.randint(jax.random.fold_in(rng, axis), (), 0, dims[axis]) for axis in range(len(dims))]
    array = array.at[tuple(place)].set(low)
    longest = dims.index(max(dims))
    place[longest] = (place[longest] + 1) % dims[longest]
    return array.at[tuple(place)].set(high)


def steps_of(stream_key, extent, shards, smallest, top_value):
    factor_of = 1.0
    for axis_at, parts in shards:
        draws = jax.random.uniform(jax.random.fold_in(jax.random.fold_in(stream_key, 6), axis_at), (parts,), jnp.float32, smallest / len(shards), top_value / len(shards))
        factor_of = factor_of * jnp.repeat(jnp.exp(draws), extent[axis_at] // parts).reshape((-1,) + (1,) * (len(extent) - 1 - axis_at))
    return factor_of


def bell_draw(stream_key, dims, spread, reach, cuts=(), kind=jnp.bfloat16):
    array = spread * jax.random.normal(stream_key, dims, jnp.float32)
    if cuts:
        array = array * steps_of(stream_key, dims, cuts, -0.22, 0.18)
    return jnp.clip(array, -reach, reach).astype(kind)


def setup_inputs(seed: int = 0) -> dict:
    splits = jax.random.split(jax.random.key(seed), 10)
    return {
        "elem_state": bell_draw(splits[0], (ELEMS, NV), 1.0, 6.0, ((0, 32),)),
        "face_metric": jnp.clip(jnp.exp(math.log(2.0) - 1.3862944 * jax.random.uniform(splits[1], (FACES, NV), jnp.float32) ** steps_of(splits[1], (FACES, NV), ((0, 32),), -0.2, 0.2)), 0.5, 2.0).astype(jnp.bfloat16),
        "right_side": draw_right_side(jax.random.fold_in(splits[9], 71), 0),
        "block_inverse": draw_block_inverse(jax.random.fold_in(splits[9], 71), 0),
        "trace_basis": bell_draw(splits[4], (NV, NV), NV ** -0.5, 0.3125),
        "flux_basis": bell_draw(splits[5], (NV, NV), NV ** -0.5, 0.3125),
        "face_rows": place_ends(jax.random.randint(splits[6], (FACES,), 0, E_DEV), jax.random.fold_in(splits[6], 1), 0, E_DEV - 1).astype(jnp.int32),
        "face_cols": place_ends(jax.random.randint(splits[7], (FACES,), 0, E_GRP), jax.random.fold_in(splits[7], 1), 0, E_GRP - 1).astype(jnp.int32),
        "face_counts": draw_face_counts(jax.random.fold_in(splits[9], 71), 0),
    }


def rounded(value):
    return lax.optimization_barrier(value.astype(jnp.bfloat16)).astype(jnp.float32)


def build_blocks(trace_basis, flux_basis, upwind, metric, live_mask):
    trace_full = trace_basis.astype(jnp.float32)
    flux_full = flux_basis.astype(jnp.float32)
    speeds = 1.0 + 0.5 * jnp.tanh(upwind.astype(jnp.float32))
    scaled = rounded(trace_full[None, :, :] * speeds[:, None, :])
    inner_prod = jnp.einsum('fik,kj->fij', scaled, flux_full)
    weighted = rounded(inner_prod * (metric.astype(jnp.float32) * live_mask[:, None])[:, None, :])
    return jnp.einsum('fik,jk->fij', weighted, trace_full).astype(jnp.bfloat16)


def reference(elem_state, face_metric, right_side, block_inverse, trace_basis, flux_basis, face_rows, face_cols, face_counts):
    device_count = N_DOM * N_FACE
    group_size = E_DEV * N_FACE
    states = elem_state.reshape(N_DOM, group_size, NV)
    row_ids = face_rows.reshape(device_count, F_DEV)
    col_ids = face_cols.reshape(device_count, F_DEV)
    metric = face_metric.reshape(device_count, F_DEV, NV)
    inverse = block_inverse.reshape(device_count, E_DEV, NV, NV)
    dom_index = jnp.arange(device_count, dtype=jnp.int32) // N_FACE
    slot_ids = jnp.arange(F_DEV, dtype=jnp.int32)
    live_mask = (slot_ids[None, :] < face_counts[:, None]).astype(jnp.float32)
    devices = jnp.arange(device_count, dtype=jnp.int32)

    def build(device):
        upwind = jnp.take(states[dom_index[device]], col_ids[device], axis=0)
        return build_blocks(trace_basis, flux_basis, upwind, metric[device], live_mask[device])

    blocks = lax.map(build, devices)

    def precondition(vectors):
        def apply_one(pair):
            inverse_block, vector_block = pair
            return jnp.einsum('eij,ej->ei', inverse_block.astype(jnp.float32), rounded(vector_block))
        return lax.map(apply_one, (inverse, vectors))

    def operate(vector):
        group_vec = rounded(vector).reshape(N_DOM, group_size, NV)

        def couple(device):
            picked = jnp.take(group_vec[dom_index[device]], col_ids[device], axis=0)
            products = jnp.einsum('fij,fj->fi', blocks[device].astype(jnp.float32), picked)
            onehot = (row_ids[device][None, :] == jnp.arange(E_DEV, dtype=jnp.int32)[:, None]).astype(jnp.float32)
            return jnp.dot(onehot, products, precision=lax.Precision.HIGHEST)

        summed = lax.map(couple, devices)
        summed = jnp.roll(summed.reshape(N_DOM, N_FACE, E_DEV, NV), 1, axis=0).reshape(device_count, E_DEV, NV)
        return vector + precondition(summed)

    start_vec = precondition(right_side.reshape(device_count, E_DEV, NV))
    first_vec = operate(start_vec)
    second_vec = operate(first_vec)
    norm_first = jnp.sum(first_vec * first_vec)
    cross_term = jnp.sum(first_vec * second_vec)
    norm_second = jnp.sum(second_vec * second_vec)
    proj_first = jnp.sum(start_vec * first_vec)
    proj_second = jnp.sum(start_vec * second_vec)
    ridge = 0.001 * (norm_first + norm_second)
    determinant = (norm_first + ridge) * (norm_second + ridge) - cross_term * cross_term
    coef_first = (proj_first * (norm_second + ridge) - proj_second * cross_term) / determinant
    coef_second = (proj_second * (norm_first + ridge) - proj_first * cross_term) / determinant
    solution = coef_first * start_vec + coef_second * first_vec
    residual = start_vec - coef_first * first_vec - coef_second * second_vec
    return solution.reshape(ELEMS, NV), residual.reshape(ELEMS, NV)
```

```python
import functools

import jax
import jax.numpy as jnp
from jax import lax
from jax.experimental import pallas as pl
from jax.experimental.pallas import tpu as pltpu
from jax.sharding import PartitionSpec as P

MESH = pl.DeviceIdType.MESH
F32 = jnp.float32
BF16 = jnp.bfloat16
LANES = 128
MAX_RADIX = 8


def radices_of(count):
    radices = []
    while count > 1:
        best = next((r for r in range(MAX_RADIX, 1, -1) if count % r == 0), None)
        if best is None:
            best = next(r for r in range(MAX_RADIX + 1, count + 1) if count % r == 0)
        radices.append(best)
        count //= best
    return radices


def nn(a, b):
    return jnp.dot(a, b, preferred_element_type=F32)


def nt(a, b):
    return lax.dot_general(a, b, (((1,), (1,)), ((), ())), preferred_element_type=F32)


def tn(a, b):
    return lax.dot_general(a, b, (((0,), (0,)), ((), ())), preferred_element_type=F32)


def two_terms(x):
    high = x.astype(BF16).astype(F32)
    return jnp.concatenate([high, x - high], axis=0).astype(BF16)


def kernel(
    n_dom,
    n_face,
    state_ref,
    metric_ref,
    rhs_ref,
    binv_hbm,
    trace_hbm,
    flux_hbm,
    rows_ref,
    cols_ref,
    count_ref,
    sol_ref,
    res_ref,
    binv,
    trace,
    flux,
    state_out,
    meta_out,
    state_in,
    metric_in,
    meta_in,
    vec_out,
    vec_in,
    sums_out,
    sums_in,
    load_sem,
    state_send,
    state_recv,
    setup_send,
    setup_recv,
    vec_send,
    vec_recv,
    sums_send,
    sums_recv,
):
    d = lax.axis_index("dom")
    f = lax.axis_index("face")
    ahead = lax.rem(d + 1, n_dom)
    behind = lax.rem(d + n_dom - 1, n_dom)
    own, nv = rhs_ref.shape
    slots = metric_ref.shape[0]
    members = own * n_face

    loads = [
        pltpu.make_async_copy(binv_hbm.at[e], binv.at[e], load_sem.at[e]) for e in range(own)
    ]
    load_trace = pltpu.make_async_copy(trace_hbm, trace, load_sem.at[own])
    load_flux = pltpu.make_async_copy(flux_hbm, flux, load_sem.at[own + 1])
    for load in loads:
        load.start()
    load_trace.start()
    load_flux.start()

    stages = []
    stages.append(
        (n_face, f, [(d, lax.rem(f + j, n_face)) for j in range(1, n_face)])
    )
    stride = 1
    for radix in radices_of(n_dom):
        digit = lax.rem(d // stride, radix)
        peers = [
            (d + (lax.rem(digit + j, radix) - digit) * stride, f) for j in range(1, radix)
        ]
        stages.append((radix, digit, peers))
        stride *= radix

    barrier = pltpu.get_barrier_semaphore()
    greeted = 0
    for peer in range(n_face):
        for dom in (ahead, behind):
            pl.semaphore_signal(barrier, inc=1, device_id=(dom, peer), device_id_type=MESH)
            greeted += 1
    for _, _, peers in stages:
        for peer in peers:
            pl.semaphore_signal(barrier, inc=1, device_id=peer, device_id_type=MESH)
            greeted += 1

    slot_ids = lax.broadcasted_iota(jnp.int32, (1, slots), 1)
    live_cols = jnp.where(slot_ids < count_ref[0], cols_ref[...], -1)
    meta_out[...] = jnp.zeros_like(meta_out)
    meta_out[0:1, 0:slots] = live_cols
    meta_out[1:2, 0:slots] = rows_ref[...]
    state_out[...] = state_ref[...].astype(F32)

    pl.semaphore_wait(barrier, greeted)

    sends = []
    sends.append(
        pltpu.make_async_remote_copy(
            meta_out, meta_in, setup_send.at[0], setup_recv.at[0], (ahead, f), MESH
        )
    )
    sends.append(
        pltpu.make_async_remote_copy(
            metric_ref, metric_in, setup_send.at[1], setup_recv.at[1], (ahead, f), MESH
        )
    )
    for peer in range(n_face):
        sends.append(
            pltpu.make_async_remote_copy(
                state_out, state_in.at[f], state_send.at[peer], state_recv.at[f], (ahead, peer), MESH
            )
        )
    for send in sends:
        send.start()

    row_ids = lax.broadcasted_iota(jnp.int32, (own, nv), 0)

    def precondition(vector):
        rounded = vector.astype(BF16).astype(F32)
        total = jnp.zeros((own, nv), F32)
        for e in range(own):
            total += nt(jnp.where(row_ids == e, rounded, 0.0).astype(BF16), binv[e])
        return total

    def send_vector(step, vector):
        vec_out[step] = vector
        for peer in range(n_face):
            copy = pltpu.make_async_remote_copy(
                vec_out.at[step],
                vec_in.at[step, f],
                vec_send.at[step, peer],
                vec_recv.at[step, f],
                (ahead, peer),
                MESH,
            )
            copy.start()
            sends.append(copy)

    for load in loads:
        load.wait()
    start_vec = precondition(rhs_ref[...])
    send_vector(0, start_vec)

    load_trace.wait()
    load_flux.wait()
    sends[0].wait_recv()
    sends[1].wait_recv()
    for peer in range(n_face):
        pltpu.make_async_remote_copy(
            state_out,
            state_in.at[peer],
            state_send.at[peer],
            state_recv.at[peer],
            (ahead, peer),
            MESH,
        ).wait_recv()
    member_ids = lax.broadcasted_iota(jnp.int32, (members, slots), 0)
    pick = (member_ids == meta_in[0:1, 0:slots]).astype(F32).astype(BF16)
    own_ids = lax.broadcasted_iota(jnp.int32, (own, slots), 0)
    gather_rows = (own_ids == meta_in[1:2, 0:slots]).astype(F32).astype(BF16)
    upwind = tn(pick, state_in[...].reshape(members, nv).astype(BF16))
    speeds = 1.0 + 0.5 * jnp.tanh(upwind)
    metric = metric_in[...].astype(F32)

    def operate(step, vector):
        for peer in range(n_face):
            pltpu.make_async_remote_copy(
                vec_out.at[step],
                vec_in.at[step, peer],
                vec_send.at[step, peer],
                vec_recv.at[step, peer],
                (ahead, peer),
                MESH,
            ).wait_recv()
        group = vec_in[step].reshape(members, nv).astype(BF16)
        picked = tn(pick, group).astype(BF16)
        lifted = nn(picked, trace[...]) * metric
        spread = nt(two_terms(lifted), flux[...])
        scaled = (spread[:slots] + spread[slots:]) * speeds
        high = scaled.astype(BF16)
        low = (scaled - high.astype(F32)).astype(BF16)
        summed = nn(gather_rows, high) + nn(gather_rows, low)
        back = nt(two_terms(summed), trace[...])
        return vector + precondition(back[:own] + back[own:])

    first_vec = operate(0, start_vec)
    send_vector(1, first_vec)
    second_vec = operate(1, first_vec)

    def lane_sums(x):
        row = jnp.sum(x, axis=0, keepdims=True)
        padded = -(-nv // LANES) * LANES
        row = jnp.concatenate([row, jnp.zeros((1, padded - nv), F32)], axis=1)
        return sum(row[:, at : at + LANES] for at in range(0, padded, LANES))

    partial = jnp.concatenate(
        [
            lane_sums(first_vec * first_vec),
            lane_sums(first_vec * second_vec),
            lane_sums(second_vec * second_vec),
            lane_sums(start_vec * first_vec),
            lane_sums(start_vec * second_vec),
            jnp.zeros((3, LANES), F32),
        ],
        axis=0,
    )
    base = 0
    for index, (radix, digit, peers) in enumerate(stages):
        sums_out[index] = partial
        for j, peer in enumerate(peers):
            copy = pltpu.make_async_remote_copy(
                sums_out.at[index],
                sums_in.at[base + j],
                sums_send.at[base + j],
                sums_recv.at[base + j],
                peer,
                MESH,
            )
            copy.start()
            sends.append(copy)
        for j, peer in enumerate(peers):
            pltpu.make_async_remote_copy(
                sums_out.at[index],
                sums_in.at[base + j],
                sums_send.at[base + j],
                sums_recv.at[base + j],
                peer,
                MESH,
            ).wait_recv()
            partial += sums_in[base + j]
        base += len(peers)

    totals = jnp.sum(partial, axis=1, keepdims=True)
    norm_first = totals[0:1]
    cross_term = totals[1:2]
    norm_second = totals[2:3]
    proj_first = totals[3:4]
    proj_second = totals[4:5]
    ridge = 0.001 * (norm_first + norm_second)
    determinant = (norm_first + ridge) * (norm_second + ridge) - cross_term * cross_term
    coef_first = (proj_first * (norm_second + ridge) - proj_second * cross_term) / determinant
    coef_second = (proj_second * (norm_first + ridge) - proj_first * cross_term) / determinant
    sol_ref[...] = coef_first * start_vec + coef_second * first_vec
    res_ref[...] = start_vec - coef_first * first_vec - coef_second * second_vec
    for send in sends:
        send.wait_send()


def on_device(
    n_dom,
    n_face,
    elem_state,
    face_metric,
    right_side,
    block_inverse,
    trace_basis,
    flux_basis,
    face_rows,
    face_cols,
    face_counts,
):
    own, nv = right_side.shape
    slots = face_rows.shape[0]
    radices = radices_of(n_dom)
    exchanges = n_face - 1 + sum(r - 1 for r in radices)
    dma = pltpu.SemaphoreType.DMA
    vmem = pl.BlockSpec(memory_space=pltpu.VMEM)
    smem = pl.BlockSpec(memory_space=pltpu.SMEM)
    hbm = pl.BlockSpec(memory_space=pl.ANY)
    return pl.pallas_call(
        functools.partial(kernel, n_dom, n_face),
        out_shape=(
            jax.ShapeDtypeStruct((own, nv), F32),
            jax.ShapeDtypeStruct((own, nv), F32),
        ),
        in_specs=[vmem, vmem, vmem, hbm, hbm, hbm, vmem, vmem, smem],
        out_specs=(vmem, vmem),
        scratch_shapes=[
            pltpu.VMEM((own, nv, nv), BF16),
            pltpu.VMEM((nv, nv), BF16),
            pltpu.VMEM((nv, nv), BF16),
            pltpu.VMEM((own, nv), F32),
            pltpu.VMEM((8, LANES), jnp.int32),
            pltpu.VMEM((n_face, own, nv), F32),
            pltpu.VMEM((slots, nv), BF16),
            pltpu.VMEM((8, LANES), jnp.int32),
            pltpu.VMEM((2, own, nv), F32),
            pltpu.VMEM((2, n_face, own, nv), F32),
            pltpu.VMEM((1 + len(radices), 8, LANES), F32),
            pltpu.VMEM((exchanges, 8, LANES), F32),
            dma((own + 2,)),
            dma((n_face,)),
            dma((n_face,)),
            dma((2,)),
            dma((2,)),
            dma((2, n_face)),
            dma((2, n_face)),
            dma((exchanges,)),
            dma((exchanges,)),
        ],
        compiler_params=pltpu.CompilerParams(
            collective_id=0, has_side_effects=True, vmem_limit_bytes=24 * 1024 * 1024
        ),
    )(
        elem_state,
        face_metric,
        right_side,
        block_inverse,
        trace_basis,
        flux_basis,
        face_rows.reshape(1, slots),
        face_cols.reshape(1, slots),
        face_counts,
    )


def solution(mesh):
    split = P(("dom", "face"))
    return jax.shard_map(
        functools.partial(on_device, mesh.shape["dom"], mesh.shape["face"]),
        mesh=mesh,
        in_specs=(
            P(("dom", "face"), None),
            P(("dom", "face"), None),
            P(("dom", "face"), None),
            P(("dom", "face"), None, None),
            P(),
            P(),
            split,
            split,
            split,
        ),
        out_specs=(P(("dom", "face"), None), P(("dom", "face"), None)),
        check_vma=False,
    )
```

```python
import functools

import jax
import jax.numpy as jnp
from jax import lax
from jax.experimental import pallas as pl
from jax.experimental.pallas import tpu as pltpu
from jax.sharding import PartitionSpec as P

MESH = pl.DeviceIdType.MESH
F32 = jnp.float32
BF16 = jnp.bfloat16
LANES = 128
MAX_RADIX = 8
PART = 256


def radices_of(count):
    radices = []
    while count > 1:
        best = next((r for r in range(MAX_RADIX, 1, -1) if count % r == 0), None)
        if best is None:
            best = next(r for r in range(MAX_RADIX + 1, count + 1) if count % r == 0)
        radices.append(best)
        count //= best
    return radices


def nn(a, b):
    return jnp.dot(a, b, preferred_element_type=F32)


def nt(a, b):
    return lax.dot_general(a, b, (((1,), (1,)), ((), ())), preferred_element_type=F32)


def tn(a, b):
    return lax.dot_general(a, b, (((0,), (0,)), ((), ())), preferred_element_type=F32)


def two_terms(x):
    high = x.astype(BF16).astype(F32)
    return jnp.concatenate([high, x - high], axis=0).astype(BF16)


def packed(x):
    right = x[:, PART:]
    right = jnp.concatenate([right, jnp.zeros((x.shape[0], 2 * PART - x.shape[1]), F32)], axis=1)
    return jnp.concatenate([x[:, :PART], right], axis=0).astype(BF16)


def await_recv(ref, send_sem, recv_sem, peer):
    pltpu.make_async_remote_copy(ref, ref, send_sem, recv_sem, peer, MESH).wait_recv()


def await_send(ref, send_sem, recv_sem, peer):
    pltpu.make_async_remote_copy(ref, ref, send_sem, recv_sem, peer, MESH).wait_send()


def kernel(
    n_dom,
    n_face,
    state_hbm,
    metric_hbm,
    rhs_hbm,
    binv_hbm,
    trace_hbm,
    flux_hbm,
    rows_hbm,
    cols_hbm,
    count_hbm,
    terms_ref,
    state,
    rhs,
    binv,
    trace,
    flux,
    rows,
    cols,
    count,
    state_out,
    state_in,
    meta_out,
    meta_in,
    metric_in,
    vec_out,
    vec_in,
    sums_out,
    sums_in,
    load_sem,
    setup_send,
    setup_recv,
    vec_send,
    vec_recv,
    sums_send,
    sums_recv,
):
    d = lax.axis_index("dom")
    f = lax.axis_index("face")
    ahead = lax.rem(d + 1, n_dom)
    behind = lax.rem(d + n_dom - 1, n_dom)
    own, nv = rhs.shape
    slots = metric_in.shape[0]

    small = [
        pltpu.make_async_copy(src, dst, load_sem.at[own + at])
        for at, (src, dst) in enumerate(
            (
                (rhs_hbm, rhs),
                (cols_hbm, cols),
                (rows_hbm, rows),
                (count_hbm, count),
                (state_hbm, state),
                (trace_hbm, trace),
                (flux_hbm, flux),
            )
        )
    ]
    loads = [
        pltpu.make_async_copy(binv_hbm.at[e], binv.at[e], load_sem.at[e]) for e in range(own)
    ]
    small[0].start()
    for load in loads:
        load.start()
    for load in small[1:]:
        load.start()

    radices = radices_of(n_dom)
    low = lax.rem(d, radices[0])
    group = n_face * radices[0]
    flat = low * n_face + f
    stages = []
    peers = []
    for j in range(1, group):
        other = lax.rem(flat + j, group)
        peers.append((d - low + other // n_face, lax.rem(other, n_face)))
    stages.append(peers)
    stride = radices[0]
    for radix in radices[1:]:
        digit = lax.rem(d // stride, radix)
        stages.append(
            [(d + (lax.rem(digit + j, radix) - digit) * stride, f) for j in range(1, radix)]
        )
        stride *= radix

    barrier = pltpu.get_barrier_semaphore()
    greeted = 0
    greet = [peer for peers in stages for peer in peers]
    if len(radices) > 1:
        greet += [(dom, peer) for peer in range(n_face) for dom in (ahead, behind)]
    for peer in greet:
        pl.semaphore_signal(barrier, inc=1, device_id=peer, device_id_type=MESH)
        greeted += 1

    row_ids = lax.broadcasted_iota(jnp.int32, (own, nv), 0)

    def precondition(vector):
        rounded = vector.astype(BF16).astype(F32)
        total = jnp.zeros((own, nv), F32)
        for e in range(own):
            total += nt(jnp.where(row_ids == e, rounded, 0.0).astype(BF16), binv[e])
        return total

    def send_vector(step):
        for peer in range(n_face):
            pltpu.make_async_remote_copy(
                vec_out.at[step],
                vec_in.at[step, f],
                vec_send.at[step],
                vec_recv.at[step],
                (ahead, peer),
                MESH,
            ).start()

    small[1].wait()
    small[2].wait()
    small[3].wait()
    small[4].wait()
    slot_ids = lax.broadcasted_iota(jnp.int32, (1, slots), 1)
    meta_out[...] = jnp.zeros_like(meta_out)
    meta_out[0:1, 0:slots] = jnp.where(slot_ids < count[...], cols[...], -1)
    meta_out[1:2, 0:slots] = rows[...]
    state_out[...] = packed(state[...].astype(F32))
    small[0].wait()
    for load in loads:
        load.wait()
    start_vec = precondition(rhs[...])
    vec_out[0] = packed(start_vec)

    pl.semaphore_wait(barrier, greeted)

    send_vector(0)
    send_meta = pltpu.make_async_remote_copy(
        meta_out, meta_in, setup_send.at[0], setup_recv.at[0], (ahead, f), MESH
    )
    send_meta.start()
    for peer in range(n_face):
        pltpu.make_async_remote_copy(
            state_out, state_in.at[f], setup_send.at[2], setup_recv.at[2], (ahead, peer), MESH
        ).start()
    send_metric = pltpu.make_async_remote_copy(
        metric_hbm, metric_in, setup_send.at[1], setup_recv.at[1], (ahead, f), MESH
    )
    send_metric.start()

    small[5].wait()
    small[6].wait()
    send_meta.wait_recv()
    own_ids = lax.broadcasted_iota(jnp.int32, (own, slots), 0)
    absent = jnp.full((own, slots), -2, jnp.int32)
    left_ids, right_ids = [], []
    for peer in range(n_face):
        left_ids += [own_ids + peer * own, absent]
        right_ids += [absent, own_ids + peer * own]
    slot_cols = meta_in[0:1, 0:slots]
    pick_left = (jnp.concatenate(left_ids, axis=0) == slot_cols).astype(F32).astype(BF16)
    pick_right = (jnp.concatenate(right_ids, axis=0) == slot_cols).astype(F32).astype(BF16)
    gather_rows = (own_ids == meta_in[1:2, 0:slots]).astype(F32).astype(BF16)

    def picked(blocks):
        stacked = blocks.reshape(n_face * 2 * own, PART)
        return tn(pick_left, stacked), tn(pick_right, stacked)[:, : nv - PART]

    def operate(step, vector):
        await_recv(vec_in.at[step], vec_send.at[step], vec_recv.at[step], (ahead, f))
        left, right = picked(vec_in[step])
        lifted = nn(left.astype(BF16), trace[0:PART]) + nn(right.astype(BF16), trace[PART:nv])
        if step == 0:
            await_recv(state_in, setup_send.at[2], setup_recv.at[2], (ahead, f))
            upwind = jnp.concatenate(picked(state_in[...]), axis=1)
            speeds.append(1.0 + 0.5 * jnp.tanh(upwind))
            send_metric.wait_recv()
        spread = nt(two_terms(lifted * metric_in[...].astype(F32)), flux[...])
        scaled = (spread[:slots] + spread[slots:]) * speeds[0]
        high = scaled.astype(BF16)
        low = (scaled - high.astype(F32)).astype(BF16)
        summed = nn(gather_rows, high) + nn(gather_rows, low)
        back = nt(two_terms(summed), trace[...])
        return vector + precondition(back[:own] + back[own:])

    speeds = []
    first_vec = operate(0, start_vec)
    vec_out[1] = packed(first_vec)
    send_vector(1)
    second_vec = operate(1, first_vec)

    lane_ids = lax.broadcasted_iota(jnp.int32, (1, LANES), 1)

    def total_at(lane, x):
        column = jnp.sum(x, axis=1, keepdims=True)
        return jnp.where(lane_ids == lane, jnp.sum(column, axis=0, keepdims=True), 0.0)

    partial = (
        total_at(0, first_vec * first_vec)
        + total_at(1, first_vec * second_vec)
        + total_at(2, second_vec * second_vec)
        + total_at(3, start_vec * first_vec)
        + total_at(4, start_vec * second_vec)
    )
    base = 0
    for index, peers in enumerate(stages):
        sums_out[index] = partial
        for j, peer in enumerate(peers):
            pltpu.make_async_remote_copy(
                sums_out.at[index],
                sums_in.at[base + j],
                sums_send.at[index],
                sums_recv.at[index],
                peer,
                MESH,
            ).start()
        landed = sums_in.at[pl.ds(base, len(peers))]
        await_recv(landed, sums_send.at[index], sums_recv.at[index], (ahead, f))
        partial += jnp.sum(sums_in[base : base + len(peers)], axis=0)
        base += len(peers)

    norm_first = partial[:, 0:1]
    cross_term = partial[:, 1:2]
    norm_second = partial[:, 2:3]
    proj_first = partial[:, 3:4]
    proj_second = partial[:, 4:5]
    ridge = 0.001 * (norm_first + norm_second)
    determinant = (norm_first + ridge) * (norm_second + ridge) - cross_term * cross_term
    coef_first = (proj_first * (norm_second + ridge) - proj_second * cross_term) / determinant
    coef_second = (proj_second * (norm_first + ridge) - proj_first * cross_term) / determinant
    terms_ref[0] = coef_first * start_vec
    terms_ref[1] = coef_second * first_vec
    terms_ref[2] = start_vec - coef_first * first_vec
    terms_ref[3] = coef_second * second_vec

    send_meta.wait_send()
    send_metric.wait_send()
    await_send(state_in, setup_send.at[2], setup_recv.at[2], (ahead, f))
    for step in range(2):
        await_send(vec_in.at[step], vec_send.at[step], vec_recv.at[step], (ahead, f))
    base = 0
    for index, peers in enumerate(stages):
        landed = sums_in.at[pl.ds(base, len(peers))]
        await_send(landed, sums_send.at[index], sums_recv.at[index], (ahead, f))
        base += len(peers)


def on_device(
    n_dom,
    n_face,
    elem_state,
    face_metric,
    right_side,
    block_inverse,
    trace_basis,
    flux_basis,
    face_rows,
    face_cols,
    face_counts,
):
    own, nv = right_side.shape
    slots = face_rows.shape[0]
    radices = radices_of(n_dom)
    exchanges = n_face * radices[0] - 1 + sum(r - 1 for r in radices[1:])
    dma = pltpu.SemaphoreType.DMA
    vmem = pl.BlockSpec(memory_space=pltpu.VMEM)
    hbm = pl.BlockSpec(memory_space=pltpu.HBM)
    terms = pl.pallas_call(
        functools.partial(kernel, n_dom, n_face),
        out_shape=jax.ShapeDtypeStruct((4, own, nv), F32),
        in_specs=[hbm] * 9,
        out_specs=vmem,
        scratch_shapes=[
            pltpu.VMEM((own, nv), BF16),
            pltpu.VMEM((own, nv), F32),
            pltpu.VMEM((own, nv, nv), BF16),
            pltpu.VMEM((nv, nv), BF16),
            pltpu.VMEM((nv, nv), BF16),
            pltpu.VMEM((1, slots), jnp.int32),
            pltpu.VMEM((1, slots), jnp.int32),
            pltpu.VMEM((1, 1), jnp.int32),
            pltpu.VMEM((2 * own, PART), BF16),
            pltpu.VMEM((n_face, 2 * own, PART), BF16),
            pltpu.VMEM((8, LANES), jnp.int32),
            pltpu.VMEM((8, LANES), jnp.int32),
            pltpu.VMEM((slots, nv), BF16),
            pltpu.VMEM((2, 2 * own, PART), BF16),
            pltpu.VMEM((2, n_face, 2 * own, PART), BF16),
            pltpu.VMEM((len(radices), 1, LANES), F32),
            pltpu.VMEM((exchanges, 1, LANES), F32),
            dma((own + 7,)),
            dma((3,)),
            dma((3,)),
            dma((2,)),
            dma((2,)),
            dma((len(radices),)),
            dma((len(radices),)),
        ],
        compiler_params=pltpu.CompilerParams(
            collective_id=0, has_side_effects=True, vmem_limit_bytes=60 * 1024 * 1024
        ),
    )(
        elem_state,
        face_metric,
        right_side,
        block_inverse,
        trace_basis,
        flux_basis,
        face_rows.reshape(1, slots),
        face_cols.reshape(1, slots),
        face_counts.reshape(1, 1),
    )
    return terms[0] + terms[1], terms[2] - terms[3]


def solution(mesh):
    split = P(("dom", "face"))
    return jax.shard_map(
        functools.partial(on_device, mesh.shape["dom"], mesh.shape["face"]),
        mesh=mesh,
        in_specs=(
            P(("dom", "face"), None),
            P(("dom", "face"), None),
            P(("dom", "face"), None),
            P(("dom", "face"), None, None),
            P(),
            P(),
            split,
            split,
            split,
        ),
        out_specs=(P(("dom", "face"), None), P(("dom", "face"), None)),
        check_vma=False,
    )
```

```python
import functools

import jax
import jax.numpy as jnp
from jax import lax
from jax.experimental import pallas as pl
from jax.experimental.pallas import tpu as pltpu
from jax.sharding import PartitionSpec as P

MESH = pl.DeviceIdType.MESH
F32 = jnp.float32
BF16 = jnp.bfloat16
LANES = 128
MAX_RADIX = 8
PART = 256


def radices_of(count):
    radices = []
    while count > 1:
        best = next((r for r in range(MAX_RADIX, 1, -1) if count % r == 0), None)
        if best is None:
            best = next(r for r in range(MAX_RADIX + 1, count + 1) if count % r == 0)
        radices.append(best)
        count //= best
    return radices


def nn(a, b):
    return jnp.dot(a, b, preferred_element_type=F32)


def nt(a, b):
    return lax.dot_general(a, b, (((1,), (1,)), ((), ())), preferred_element_type=F32)


def tn(a, b):
    return lax.dot_general(a, b, (((0,), (0,)), ((), ())), preferred_element_type=F32)


def two_terms(x):
    high = x.astype(BF16).astype(F32)
    return jnp.concatenate([high, x - high], axis=0).astype(BF16)


def packed(x):
    right = x[:, PART:]
    right = jnp.concatenate([right, jnp.zeros((x.shape[0], 2 * PART - x.shape[1]), F32)], axis=1)
    return jnp.concatenate([x[:, :PART], right], axis=0).astype(BF16)


def await_recv(ref, send_sem, recv_sem, peer):
    pltpu.make_async_remote_copy(ref, ref, send_sem, recv_sem, peer, MESH).wait_recv()


def await_send(ref, send_sem, recv_sem, peer):
    pltpu.make_async_remote_copy(ref, ref, send_sem, recv_sem, peer, MESH).wait_send()


def kernel(
    n_dom,
    n_face,
    state_hbm,
    metric_hbm,
    rhs_hbm,
    binv_hbm,
    trace_hbm,
    flux_hbm,
    rows_hbm,
    cols_hbm,
    count_hbm,
    terms_ref,
    state,
    rhs,
    binv,
    solved,
    trace,
    trace_turned,
    flux,
    flux_turned,
    rows,
    cols,
    count,
    state_out,
    state_in,
    meta_out,
    meta_in,
    metric_in,
    vec_out,
    vec_in,
    sums_out,
    sums_in,
    load_sem,
    setup_send,
    setup_recv,
    vec_send,
    vec_recv,
    sums_send,
    sums_recv,
):
    d = lax.axis_index("dom")
    f = lax.axis_index("face")
    ahead = lax.rem(d + 1, n_dom)
    behind = lax.rem(d + n_dom - 1, n_dom)
    own, nv = rhs.shape
    slots = metric_in.shape[0]

    small = [
        pltpu.make_async_copy(src, dst, load_sem.at[own + at])
        for at, (src, dst) in enumerate(
            (
                (rhs_hbm, rhs),
                (cols_hbm, cols),
                (rows_hbm, rows),
                (count_hbm, count),
                (state_hbm, state),
                (trace_hbm, trace),
                (flux_hbm, flux),
            )
        )
    ]
    loads = [
        pltpu.make_async_copy(binv_hbm.at[e], binv.at[e], load_sem.at[e]) for e in range(own)
    ]
    small[0].start()
    for load in loads:
        load.start()
    for load in small[1:]:
        load.start()

    radices = radices_of(n_dom)
    low = lax.rem(d, radices[0])
    group = n_face * radices[0]
    flat = low * n_face + f
    stages = []
    peers = []
    for j in range(1, group):
        other = lax.rem(flat + j, group)
        peers.append((d - low + other // n_face, lax.rem(other, n_face)))
    stages.append(peers)
    stride = radices[0]
    for radix in radices[1:]:
        digit = lax.rem(d // stride, radix)
        stages.append(
            [(d + (lax.rem(digit + j, radix) - digit) * stride, f) for j in range(1, radix)]
        )
        stride *= radix

    barrier = pltpu.get_barrier_semaphore()
    greeted = 0
    greet = [peer for peers in stages for peer in peers]
    if len(radices) > 1:
        greet += [(dom, peer) for peer in range(n_face) for dom in (ahead, behind)]
    for peer in greet:
        pl.semaphore_signal(barrier, inc=1, device_id=peer, device_id_type=MESH)
        greeted += 1

    row_ids = lax.broadcasted_iota(jnp.int32, (own, nv), 0)

    def precondition(vector):
        rounded = vector.astype(BF16).astype(F32)
        total = jnp.zeros((own, nv), F32)
        for e in range(own):
            total += nt(jnp.where(row_ids == e, rounded, 0.0).astype(BF16), binv[e])
        return total

    def lift_and_precondition(vector):
        high = vector.astype(BF16).astype(F32)
        terms = jnp.concatenate([high, vector - high], axis=0)
        term_ids = jnp.concatenate([row_ids, row_ids], axis=0)
        total = jnp.zeros((2 * own, nv), F32)
        for e in range(own):
            total += nn(jnp.where(term_ids == e, terms, 0.0).astype(BF16), solved[e])
        return total[:own] + total[own:]

    def send_vector(step):
        for peer in range(n_face):
            pltpu.make_async_remote_copy(
                vec_out.at[step],
                vec_in.at[step, f],
                vec_send.at[step],
                vec_recv.at[step],
                (ahead, peer),
                MESH,
            ).start()

    small[1].wait()
    small[2].wait()
    small[3].wait()
    small[4].wait()
    slot_ids = lax.broadcasted_iota(jnp.int32, (1, slots), 1)
    meta_out[...] = jnp.zeros_like(meta_out)
    meta_out[0:1, 0:slots] = jnp.where(slot_ids < count[...], cols[...], -1)
    meta_out[1:2, 0:slots] = rows[...]
    state_out[...] = packed(state[...].astype(F32))
    small[0].wait()
    for load in loads:
        load.wait()
    start_vec = precondition(rhs[...])
    vec_out[0] = packed(start_vec)

    pl.semaphore_wait(barrier, greeted)

    send_vector(0)
    send_meta = pltpu.make_async_remote_copy(
        meta_out, meta_in, setup_send.at[0], setup_recv.at[0], (ahead, f), MESH
    )
    send_meta.start()
    for peer in range(n_face):
        pltpu.make_async_remote_copy(
            state_out, state_in.at[f], setup_send.at[2], setup_recv.at[2], (ahead, peer), MESH
        ).start()
    send_metric = pltpu.make_async_remote_copy(
        metric_hbm, metric_in, setup_send.at[1], setup_recv.at[1], (ahead, f), MESH
    )
    send_metric.start()

    small[5].wait()
    small[6].wait()
    flux_turned[...] = flux[...].T
    trace_turned[...] = trace[...].T
    for e in range(own):
        solved[e] = nt(trace_turned[...], binv[e]).astype(BF16)

    send_meta.wait_recv()
    own_ids = lax.broadcasted_iota(jnp.int32, (own, slots), 0)
    absent = jnp.full((own, slots), -2, jnp.int32)
    left_ids, right_ids = [], []
    for peer in range(n_face):
        left_ids += [own_ids + peer * own, absent]
        right_ids += [absent, own_ids + peer * own]
    slot_cols = meta_in[0:1, 0:slots]
    pick_left = (jnp.concatenate(left_ids, axis=0) == slot_cols).astype(F32).astype(BF16)
    pick_right = (jnp.concatenate(right_ids, axis=0) == slot_cols).astype(F32).astype(BF16)
    gather_rows = (own_ids == meta_in[1:2, 0:slots]).astype(F32)
    gather_rows = jnp.concatenate([gather_rows, gather_rows], axis=1).astype(BF16)

    def picked(blocks):
        stacked = blocks.reshape(n_face * 2 * own, PART)
        return tn(pick_left, stacked), tn(pick_right, stacked)[:, : nv - PART]

    def operate(step, vector):
        await_recv(vec_in.at[step], vec_send.at[step], vec_recv.at[step], (ahead, f))
        left, right = picked(vec_in[step])
        lifted = nn(left.astype(BF16), trace[0:PART]) + nn(right.astype(BF16), trace[PART:nv])
        if step == 0:
            await_recv(state_in, setup_send.at[2], setup_recv.at[2], (ahead, f))
            upwind = jnp.concatenate(picked(state_in[...]), axis=1)
            speeds.append(1.0 + 0.5 * jnp.tanh(upwind))
            send_metric.wait_recv()
        spread = nn(two_terms(lifted * metric_in[...].astype(F32)), flux_turned[...])
        scaled = (spread[:slots] + spread[slots:]) * speeds[0]
        summed = nn(gather_rows, two_terms(scaled))
        return vector + lift_and_precondition(summed)

    speeds = []
    first_vec = operate(0, start_vec)
    vec_out[1] = packed(first_vec)
    send_vector(1)
    second_vec = operate(1, first_vec)

    lane_ids = lax.broadcasted_iota(jnp.int32, (1, LANES), 1)

    def total_at(lane, x):
        column = jnp.sum(x, axis=1, keepdims=True)
        return jnp.where(lane_ids == lane, jnp.sum(column, axis=0, keepdims=True), 0.0)

    partial = (
        total_at(0, first_vec * first_vec)
        + total_at(1, first_vec * second_vec)
        + total_at(2, second_vec * second_vec)
        + total_at(3, start_vec * first_vec)
        + total_at(4, start_vec * second_vec)
    )
    base = 0
    for index, peers in enumerate(stages):
        sums_out[index] = partial
        for j, peer in enumerate(peers):
            pltpu.make_async_remote_copy(
                sums_out.at[index],
                sums_in.at[base + j],
                sums_send.at[index],
                sums_recv.at[index],
                peer,
                MESH,
            ).start()
        landed = sums_in.at[pl.ds(base, len(peers))]
        await_recv(landed, sums_send.at[index], sums_recv.at[index], (ahead, f))
        partial += jnp.sum(sums_in[base : base + len(peers)], axis=0)
        base += len(peers)

    norm_first = partial[:, 0:1]
    cross_term = partial[:, 1:2]
    norm_second = partial[:, 2:3]
    proj_first = partial[:, 3:4]
    proj_second = partial[:, 4:5]
    ridge = 0.001 * (norm_first + norm_second)
    determinant = (norm_first + ridge) * (norm_second + ridge) - cross_term * cross_term
    coef_first = (proj_first * (norm_second + ridge) - proj_second * cross_term) / determinant
    coef_second = (proj_second * (norm_first + ridge) - proj_first * cross_term) / determinant
    terms_ref[0] = coef_first * start_vec
    terms_ref[1] = coef_second * first_vec
    terms_ref[2] = start_vec - coef_first * first_vec
    terms_ref[3] = coef_second * second_vec

    send_meta.wait_send()
    send_metric.wait_send()
    await_send(state_in, setup_send.at[2], setup_recv.at[2], (ahead, f))
    for step in range(2):
        await_send(vec_in.at[step], vec_send.at[step], vec_recv.at[step], (ahead, f))
    base = 0
    for index, peers in enumerate(stages):
        landed = sums_in.at[pl.ds(base, len(peers))]
        await_send(landed, sums_send.at[index], sums_recv.at[index], (ahead, f))
        base += len(peers)


def on_device(
    n_dom,
    n_face,
    elem_state,
    face_metric,
    right_side,
    block_inverse,
    trace_basis,
    flux_basis,
    face_rows,
    face_cols,
    face_counts,
):
    own, nv = right_side.shape
    slots = face_rows.shape[0]
    radices = radices_of(n_dom)
    exchanges = n_face * radices[0] - 1 + sum(r - 1 for r in radices[1:])
    dma = pltpu.SemaphoreType.DMA
    vmem = pl.BlockSpec(memory_space=pltpu.VMEM)
    hbm = pl.BlockSpec(memory_space=pltpu.HBM)
    terms = pl.pallas_call(
        functools.partial(kernel, n_dom, n_face),
        out_shape=pltpu.VMEM((4, own, nv), F32),
        in_specs=[hbm] * 9,
        out_specs=vmem,
        scratch_shapes=[
            pltpu.VMEM((own, nv), BF16),
            pltpu.VMEM((own, nv), F32),
            pltpu.VMEM((own, nv, nv), BF16),
            pltpu.VMEM((own, nv, nv), BF16),
            pltpu.VMEM((nv, nv), BF16),
            pltpu.VMEM((nv, nv), BF16),
            pltpu.VMEM((nv, nv), BF16),
            pltpu.VMEM((nv, nv), BF16),
            pltpu.VMEM((1, slots), jnp.int32),
            pltpu.VMEM((1, slots), jnp.int32),
            pltpu.VMEM((1, 1), jnp.int32),
            pltpu.VMEM((2 * own, PART), BF16),
            pltpu.VMEM((n_face, 2 * own, PART), BF16),
            pltpu.VMEM((8, LANES), jnp.int32),
            pltpu.VMEM((8, LANES), jnp.int32),
            pltpu.VMEM((slots, nv), BF16),
            pltpu.VMEM((2, 2 * own, PART), BF16),
            pltpu.VMEM((2, n_face, 2 * own, PART), BF16),
            pltpu.VMEM((len(radices), 1, LANES), F32),
            pltpu.VMEM((exchanges, 1, LANES), F32),
            dma((own + 7,)),
            dma((3,)),
            dma((3,)),
            dma((2,)),
            dma((2,)),
            dma((len(radices),)),
            dma((len(radices),)),
        ],
        compiler_params=pltpu.CompilerParams(
            collective_id=0, has_side_effects=True, vmem_limit_bytes=24 * 1024 * 1024
        ),
    )(
        *(
            pltpu.with_memory_space_constraint(operand, pltpu.HBM)
            for operand in (
                elem_state,
                face_metric,
                right_side,
                block_inverse,
                trace_basis,
                flux_basis,
                face_rows.reshape(1, slots),
                face_cols.reshape(1, slots),
            )
        ),
        face_counts.reshape(1, 1),
    )
    return terms[0] + terms[1], terms[2] - terms[3]


def solution(mesh):
    split = P(("dom", "face"))
    return jax.shard_map(
        functools.partial(on_device, mesh.shape["dom"], mesh.shape["face"]),
        mesh=mesh,
        in_specs=(
            P(("dom", "face"), None),
            P(("dom", "face"), None),
            P(("dom", "face"), None),
            P(("dom", "face"), None, None),
            P(),
            P(),
            split,
            split,
            split,
        ),
        out_specs=(P(("dom", "face"), None), P(("dom", "face"), None)),
        check_vma=False,
    )
```

```python
import functools

import jax
import jax.numpy as jnp
from jax import lax
from jax.experimental import pallas as pl
from jax.experimental.pallas import tpu as pltpu
from jax.sharding import PartitionSpec as P

MESH = pl.DeviceIdType.MESH
F32 = jnp.float32
BF16 = jnp.bfloat16
LANES = 128
MAX_RADIX = 8
PART = 256


def radices_of(count):
    radices = []
    while count > 1:
        best = next((r for r in range(MAX_RADIX, 1, -1) if count % r == 0), None)
        if best is None:
            best = next(r for r in range(MAX_RADIX + 1, count + 1) if count % r == 0)
        radices.append(best)
        count //= best
    return radices


def nn(a, b):
    return jnp.dot(a, b, preferred_element_type=F32)


def nt(a, b):
    return lax.dot_general(a, b, (((1,), (1,)), ((), ())), preferred_element_type=F32)


def two_terms(x):
    high = x.astype(BF16).astype(F32)
    return jnp.concatenate([high, x - high], axis=0).astype(BF16)


def packed(x):
    right = x[:, PART:]
    right = jnp.concatenate([right, jnp.zeros((x.shape[0], 2 * PART - x.shape[1]), F32)], axis=1)
    return jnp.concatenate([x[:, :PART], right], axis=0).astype(BF16)


def await_recv(ref, send_sem, recv_sem, peer):
    pltpu.make_async_remote_copy(ref, ref, send_sem, recv_sem, peer, MESH).wait_recv()


def await_send(ref, send_sem, recv_sem, peer):
    pltpu.make_async_remote_copy(ref, ref, send_sem, recv_sem, peer, MESH).wait_send()


def kernel(
    n_dom,
    n_face,
    state_hbm,
    metric_hbm,
    rhs_hbm,
    binv_hbm,
    trace_hbm,
    flux_hbm,
    rows_hbm,
    cols_hbm,
    count_hbm,
    terms_ref,
    state,
    rhs,
    binv,
    solved,
    trace,
    trace_turned,
    flux,
    flux_turned,
    rows,
    cols,
    count,
    state_out,
    state_in,
    meta_out,
    meta_in,
    metric_in,
    vec_out,
    vec_in,
    sums_out,
    sums_in,
    load_sem,
    setup_send,
    setup_recv,
    vec_send,
    vec_recv,
    sums_send,
    sums_recv,
):
    d = lax.axis_index("dom")
    f = lax.axis_index("face")
    ahead = lax.rem(d + 1, n_dom)
    behind = lax.rem(d + n_dom - 1, n_dom)
    own, nv = rhs.shape
    slots = metric_in.shape[0]

    small = [
        pltpu.make_async_copy(src, dst, load_sem.at[own + at])
        for at, (src, dst) in enumerate(
            (
                (rhs_hbm, rhs),
                (cols_hbm, cols),
                (rows_hbm, rows),
                (count_hbm, count),
                (state_hbm, state),
                (trace_hbm, trace),
                (flux_hbm, flux),
            )
        )
    ]
    loads = [
        pltpu.make_async_copy(binv_hbm.at[e], binv.at[e], load_sem.at[e]) for e in range(own)
    ]
    for load in small[:5] + loads + small[5:]:
        load.start()

    radices = radices_of(n_dom)
    low = lax.rem(d, radices[0])
    group = n_face * radices[0]
    flat = low * n_face + f
    stages = []
    peers = []
    for j in range(1, group):
        other = lax.rem(flat + j, group)
        peers.append((d - low + other // n_face, lax.rem(other, n_face)))
    stages.append(peers)
    stride = radices[0]
    for radix in radices[1:]:
        digit = lax.rem(d // stride, radix)
        stages.append(
            [(d + (lax.rem(digit + j, radix) - digit) * stride, f) for j in range(1, radix)]
        )
        stride *= radix

    barrier = pltpu.get_barrier_semaphore()
    greeted = 0
    greet = [peer for peers in stages for peer in peers]
    if len(radices) > 1:
        greet += [(dom, peer) for peer in range(n_face) for dom in (ahead, behind)]
    for peer in greet:
        pl.semaphore_signal(barrier, inc=1, device_id=peer, device_id_type=MESH)
        greeted += 1

    row_ids = lax.broadcasted_iota(jnp.int32, (own, nv), 0)

    def precondition(vector):
        rounded = vector.astype(BF16).astype(F32)
        total = jnp.zeros((own, nv), F32)
        for e in range(own):
            loads[e].wait()
            total += nt(jnp.where(row_ids == e, rounded, 0.0).astype(BF16), binv[e])
        return total

    def lift_and_precondition(vector):
        high = vector.astype(BF16).astype(F32)
        terms = jnp.concatenate([high, vector - high], axis=0)
        term_ids = jnp.concatenate([row_ids, row_ids], axis=0)
        total = jnp.zeros((2 * own, nv), F32)
        for e in range(own):
            total += nn(jnp.where(term_ids == e, terms, 0.0).astype(BF16), solved[e])
        return total[:own] + total[own:]

    def send_vector(step):
        for peer in range(n_face):
            pltpu.make_async_remote_copy(
                vec_out.at[step],
                vec_in.at[step, f],
                vec_send.at[step],
                vec_recv.at[step],
                (ahead, peer),
                MESH,
            ).start()

    small[1].wait()
    small[2].wait()
    small[3].wait()
    small[4].wait()
    slot_ids = lax.broadcasted_iota(jnp.int32, (1, slots), 1)
    meta_out[...] = jnp.zeros_like(meta_out)
    meta_out[0:1, 0:slots] = jnp.where(slot_ids < count[...], cols[...], -1)
    meta_out[1:2, 0:slots] = rows[...]
    state_out[...] = packed(state[...].astype(F32))

    pl.semaphore_wait(barrier, greeted)

    send_meta = pltpu.make_async_remote_copy(
        meta_out, meta_in, setup_send.at[0], setup_recv.at[0], (ahead, f), MESH
    )
    send_meta.start()
    for peer in range(n_face):
        pltpu.make_async_remote_copy(
            state_out, state_in.at[f], setup_send.at[2], setup_recv.at[2], (ahead, peer), MESH
        ).start()
    send_metric = pltpu.make_async_remote_copy(
        metric_hbm, metric_in, setup_send.at[1], setup_recv.at[1], (ahead, f), MESH
    )
    send_metric.start()

    small[0].wait()
    start_vec = precondition(rhs[...])
    vec_out[0] = packed(start_vec)
    send_vector(0)

    small[5].wait()
    small[6].wait()
    flux_turned[...] = flux[...].T
    trace_turned[...] = trace[...].T
    for e in range(own):
        solved[e] = nt(trace_turned[...], binv[e]).astype(BF16)

    send_meta.wait_recv()
    own_ids = lax.broadcasted_iota(jnp.int32, (own, slots), 0)
    absent = jnp.full((own, slots), -2, jnp.int32)
    left_ids, right_ids = [], []
    for peer in range(n_face):
        left_ids += [own_ids + peer * own, absent]
        right_ids += [absent, own_ids + peer * own]
    slot_cols = meta_in[0:1, 0:slots]
    pick_left = (jnp.concatenate(left_ids, axis=0) == slot_cols).astype(F32)
    pick_right = (jnp.concatenate(right_ids, axis=0) == slot_cols).astype(F32)
    pick = jnp.concatenate([pick_left, pick_right], axis=1).T.astype(BF16)
    gather_rows = (own_ids == meta_in[1:2, 0:slots]).astype(F32)
    gather_rows = jnp.concatenate([gather_rows, gather_rows], axis=1).astype(BF16)

    def picked(blocks):
        both = nn(pick, blocks.reshape(n_face * 2 * own, PART))
        return both[:slots], both[slots:, : nv - PART]

    await_recv(state_in, setup_send.at[2], setup_recv.at[2], (ahead, f))
    speeds = 1.0 + 0.5 * jnp.tanh(jnp.concatenate(picked(state_in[...]), axis=1))
    send_metric.wait_recv()

    def operate(step, vector):
        await_recv(vec_in.at[step], vec_send.at[step], vec_recv.at[step], (ahead, f))
        left, right = picked(vec_in[step])
        lifted = nn(left.astype(BF16), trace[0:PART]) + nn(right.astype(BF16), trace[PART:nv])
        spread = nn(two_terms(lifted * metric_in[...].astype(F32)), flux_turned[...])
        scaled = (spread[:slots] + spread[slots:]) * speeds
        summed = nn(gather_rows, two_terms(scaled))
        return vector + lift_and_precondition(summed)

    first_vec = operate(0, start_vec)
    vec_out[1] = packed(first_vec)
    send_vector(1)
    lane_ids = lax.broadcasted_iota(jnp.int32, (1, LANES), 1)

    def total_at(lane, x):
        column = jnp.sum(x, axis=1, keepdims=True)
        return jnp.where(lane_ids == lane, jnp.sum(column, axis=0, keepdims=True), 0.0)

    early = total_at(0, first_vec * first_vec) + total_at(3, start_vec * first_vec)
    second_vec = operate(1, first_vec)

    partial = (
        early
        + total_at(1, first_vec * second_vec)
        + total_at(2, second_vec * second_vec)
        + total_at(4, start_vec * second_vec)
    )
    base = 0
    for index, peers in enumerate(stages):
        sums_out[index] = partial
        for j, peer in enumerate(peers):
            pltpu.make_async_remote_copy(
                sums_out.at[index],
                sums_in.at[base + j],
                sums_send.at[index],
                sums_recv.at[index],
                peer,
                MESH,
            ).start()
        landed = sums_in.at[pl.ds(base, len(peers))]
        await_recv(landed, sums_send.at[index], sums_recv.at[index], (ahead, f))
        partial += jnp.sum(sums_in[base : base + len(peers)], axis=0)
        base += len(peers)

    norm_first = partial[:, 0:1]
    cross_term = partial[:, 1:2]
    norm_second = partial[:, 2:3]
    proj_first = partial[:, 3:4]
    proj_second = partial[:, 4:5]
    ridge = 0.001 * (norm_first + norm_second)
    determinant = (norm_first + ridge) * (norm_second + ridge) - cross_term * cross_term
    coef_first = (proj_first * (norm_second + ridge) - proj_second * cross_term) / determinant
    coef_second = (proj_second * (norm_first + ridge) - proj_first * cross_term) / determinant
    terms_ref[0] = coef_first * start_vec
    terms_ref[1] = coef_second * first_vec
    terms_ref[2] = start_vec - coef_first * first_vec
    terms_ref[3] = coef_second * second_vec

    send_meta.wait_send()
    send_metric.wait_send()
    await_send(state_in, setup_send.at[2], setup_recv.at[2], (ahead, f))
    for step in range(2):
        await_send(vec_in.at[step], vec_send.at[step], vec_recv.at[step], (ahead, f))
    base = 0
    for index, peers in enumerate(stages):
        landed = sums_in.at[pl.ds(base, len(peers))]
        await_send(landed, sums_send.at[index], sums_recv.at[index], (ahead, f))
        base += len(peers)


def on_device(
    n_dom,
    n_face,
    elem_state,
    face_metric,
    right_side,
    block_inverse,
    trace_basis,
    flux_basis,
    face_rows,
    face_cols,
    face_counts,
):
    own, nv = right_side.shape
    slots = face_rows.shape[0]
    radices = radices_of(n_dom)
    exchanges = n_face * radices[0] - 1 + sum(r - 1 for r in radices[1:])
    dma = pltpu.SemaphoreType.DMA
    vmem = pl.BlockSpec(memory_space=pltpu.VMEM)
    hbm = pl.BlockSpec(memory_space=pltpu.HBM)
    terms = pl.pallas_call(
        functools.partial(kernel, n_dom, n_face),
        out_shape=pltpu.VMEM((4, own, nv), F32),
        in_specs=[hbm] * 9,
        out_specs=vmem,
        scratch_shapes=[
            pltpu.VMEM((own, nv), BF16),
            pltpu.VMEM((own, nv), F32),
            pltpu.VMEM((own, nv, nv), BF16),
            pltpu.VMEM((own, nv, nv), BF16),
            pltpu.VMEM((nv, nv), BF16),
            pltpu.VMEM((nv, nv), BF16),
            pltpu.VMEM((nv, nv), BF16),
            pltpu.VMEM((nv, nv), BF16),
            pltpu.VMEM((1, slots), jnp.int32),
            pltpu.VMEM((1, slots), jnp.int32),
            pltpu.VMEM((1, 1), jnp.int32),
            pltpu.VMEM((2 * own, PART), BF16),
            pltpu.VMEM((n_face, 2 * own, PART), BF16),
            pltpu.VMEM((8, LANES), jnp.int32),
            pltpu.VMEM((8, LANES), jnp.int32),
            pltpu.VMEM((slots, nv), BF16),
            pltpu.VMEM((2, 2 * own, PART), BF16),
            pltpu.VMEM((2, n_face, 2 * own, PART), BF16),
            pltpu.VMEM((len(radices), 1, LANES), F32),
            pltpu.VMEM((exchanges, 1, LANES), F32),
            dma((own + 7,)),
            dma((3,)),
            dma((3,)),
            dma((2,)),
            dma((2,)),
            dma((len(radices),)),
            dma((len(radices),)),
        ],
        compiler_params=pltpu.CompilerParams(
            collective_id=0, has_side_effects=True, vmem_limit_bytes=24 * 1024 * 1024
        ),
    )(
        *(
            pltpu.with_memory_space_constraint(operand, pltpu.HBM)
            for operand in (
                elem_state,
                face_metric,
                right_side,
                block_inverse,
                trace_basis,
                flux_basis,
                face_rows.reshape(1, slots),
                face_cols.reshape(1, slots),
            )
        ),
        face_counts.reshape(1, 1),
    )
    return terms[0] + terms[1], terms[2] - terms[3]


def solution(mesh):
    split = P(("dom", "face"))
    return jax.shard_map(
        functools.partial(on_device, mesh.shape["dom"], mesh.shape["face"]),
        mesh=mesh,
        in_specs=(
            P(("dom", "face"), None),
            P(("dom", "face"), None),
            P(("dom", "face"), None),
            P(("dom", "face"), None, None),
            P(),
            P(),
            split,
            split,
            split,
        ),
        out_specs=(P(("dom", "face"), None), P(("dom", "face"), None)),
        check_vma=False,
    )
```

```python
import functools

import jax
import jax.numpy as jnp
from jax import lax
from jax.experimental import pallas as pl
from jax.experimental.pallas import tpu as pltpu
from jax.sharding import PartitionSpec as P

MESH = pl.DeviceIdType.MESH
F32 = jnp.float32
BF16 = jnp.bfloat16
LANES = 128
MAX_RADIX = 8
PART = 256


def radices_of(count):
    radices = []
    while count > 1:
        best = next((r for r in range(MAX_RADIX, 1, -1) if count % r == 0), None)
        if best is None:
            best = next(r for r in range(MAX_RADIX + 1, count + 1) if count % r == 0)
        radices.append(best)
        count //= best
    return radices


def nn(a, b):
    return jnp.dot(a, b, preferred_element_type=F32)


def nt(a, b):
    return lax.dot_general(a, b, (((1,), (1,)), ((), ())), preferred_element_type=F32)


def two_terms(x):
    high = x.astype(BF16).astype(F32)
    return jnp.concatenate([high, x - high], axis=0).astype(BF16)


def packed(x):
    right = x[:, PART:]
    right = jnp.concatenate([right, jnp.zeros((x.shape[0], 2 * PART - x.shape[1]), F32)], axis=1)
    return jnp.concatenate([x[:, :PART], right], axis=0).astype(BF16)


def await_recv(ref, send_sem, recv_sem, peer):
    pltpu.make_async_remote_copy(ref, ref, send_sem, recv_sem, peer, MESH).wait_recv()


def await_send(ref, send_sem, recv_sem, peer):
    pltpu.make_async_remote_copy(ref, ref, send_sem, recv_sem, peer, MESH).wait_send()


def kernel(
    n_dom,
    n_face,
    state_hbm,
    metric_hbm,
    rhs_hbm,
    binv_hbm,
    trace_hbm,
    flux_hbm,
    rows_hbm,
    cols_hbm,
    count_hbm,
    terms_ref,
    state,
    rhs,
    binv,
    solved,
    trace,
    trace_turned,
    flux,
    flux_turned,
    rows,
    cols,
    count,
    state_out,
    state_in,
    meta_out,
    meta_in,
    metric_in,
    vec_out,
    vec_in,
    sums_out,
    sums_in,
    load_sem,
    setup_send,
    setup_recv,
    vec_send,
    vec_recv,
    sums_send,
    sums_recv,
):
    d = lax.axis_index("dom")
    f = lax.axis_index("face")
    ahead = lax.rem(d + 1, n_dom)
    behind = lax.rem(d + n_dom - 1, n_dom)
    own, nv = rhs.shape
    slots = metric_in.shape[0]

    small = [
        pltpu.make_async_copy(src, dst, load_sem.at[own + at])
        for at, (src, dst) in enumerate(
            (
                (rhs_hbm, rhs),
                (cols_hbm, cols),
                (rows_hbm, rows),
                (count_hbm, count),
                (state_hbm, state),
                (trace_hbm, trace),
                (flux_hbm, flux),
            )
        )
    ]
    loads = [
        pltpu.make_async_copy(binv_hbm.at[e], binv.at[e], load_sem.at[e]) for e in range(own)
    ]
    for load in small[:5] + loads + small[5:]:
        load.start()

    radices = radices_of(n_dom)
    stages = [[(d, lax.rem(f + j, n_face)) for j in range(1, n_face)]]
    stride = 1
    for radix in radices:
        digit = lax.rem(d // stride, radix)
        stages.append(
            [(d + (lax.rem(digit + j, radix) - digit) * stride, f) for j in range(1, radix)]
        )
        stride *= radix

    barrier = pltpu.get_barrier_semaphore()
    greeted = 0
    greet = [peer for peers in stages for peer in peers]
    greet += [(dom, peer) for peer in range(n_face) for dom in (ahead, behind)]
    for peer in greet:
        pl.semaphore_signal(barrier, inc=1, device_id=peer, device_id_type=MESH)
        greeted += 1

    row_ids = lax.broadcasted_iota(jnp.int32, (own, nv), 0)

    def precondition(vector):
        rounded = vector.astype(BF16).astype(F32)
        total = jnp.zeros((own, nv), F32)
        for e in range(own):
            loads[e].wait()
            total += nt(jnp.where(row_ids == e, rounded, 0.0).astype(BF16), binv[e])
        return total

    def lift_and_precondition(vector):
        high = vector.astype(BF16).astype(F32)
        terms = jnp.concatenate([high, vector - high], axis=0)
        term_ids = jnp.concatenate([row_ids, row_ids], axis=0)
        total = jnp.zeros((2 * own, nv), F32)
        for e in range(own):
            total += nn(jnp.where(term_ids == e, terms, 0.0).astype(BF16), solved[e])
        return total[:own] + total[own:]

    def send_vector(step):
        for peer in range(n_face):
            pltpu.make_async_remote_copy(
                vec_out.at[step],
                vec_in.at[step, f],
                vec_send.at[step],
                vec_recv.at[step],
                (ahead, peer),
                MESH,
            ).start()

    small[1].wait()
    small[2].wait()
    small[3].wait()
    small[4].wait()
    slot_ids = lax.broadcasted_iota(jnp.int32, (1, slots), 1)
    meta_out[...] = jnp.zeros_like(meta_out)
    meta_out[0:1, 0:slots] = jnp.where(slot_ids < count[...], cols[...], -1)
    meta_out[1:2, 0:slots] = rows[...]
    state_out[...] = packed(state[...].astype(F32))

    pl.semaphore_wait(barrier, greeted)

    send_meta = pltpu.make_async_remote_copy(
        meta_out, meta_in, setup_send.at[0], setup_recv.at[0], (ahead, f), MESH
    )
    send_meta.start()
    for peer in range(n_face):
        pltpu.make_async_remote_copy(
            state_out, state_in.at[f], setup_send.at[2], setup_recv.at[2], (ahead, peer), MESH
        ).start()
    send_metric = pltpu.make_async_remote_copy(
        metric_hbm, metric_in, setup_send.at[1], setup_recv.at[1], (ahead, f), MESH
    )
    send_metric.start()

    small[0].wait()
    start_vec = precondition(rhs[...])
    vec_out[0] = packed(start_vec)
    send_vector(0)

    small[5].wait()
    small[6].wait()
    flux_turned[...] = flux[...].T
    trace_turned[...] = trace[...].T
    for e in range(own):
        solved[e] = nt(trace_turned[...], binv[e]).astype(BF16)

    send_meta.wait_recv()
    own_ids = lax.broadcasted_iota(jnp.int32, (own, slots), 0)
    absent = jnp.full((own, slots), -2, jnp.int32)
    left_ids, right_ids = [], []
    for peer in range(n_face):
        left_ids += [own_ids + peer * own, absent]
        right_ids += [absent, own_ids + peer * own]
    slot_cols = meta_in[0:1, 0:slots]
    pick_left = (jnp.concatenate(left_ids, axis=0) == slot_cols).astype(F32)
    pick_right = (jnp.concatenate(right_ids, axis=0) == slot_cols).astype(F32)
    pick = jnp.concatenate([pick_left, pick_right], axis=1).T.astype(BF16)
    gather_rows = (own_ids == meta_in[1:2, 0:slots]).astype(F32)
    gather_rows = jnp.concatenate([gather_rows, gather_rows], axis=1).astype(BF16)

    def picked(blocks):
        both = nn(pick, blocks.reshape(n_face * 2 * own, PART))
        return both[:slots], both[slots:, : nv - PART]

    await_recv(state_in, setup_send.at[2], setup_recv.at[2], (ahead, f))
    speeds = 1.0 + 0.5 * jnp.tanh(jnp.concatenate(picked(state_in[...]), axis=1))
    send_metric.wait_recv()

    def operate(step, vector):
        await_recv(vec_in.at[step], vec_send.at[step], vec_recv.at[step], (ahead, f))
        left, right = picked(vec_in[step])
        lifted = nn(left.astype(BF16), trace[0:PART]) + nn(right.astype(BF16), trace[PART:nv])
        spread = nn(two_terms(lifted * metric_in[...].astype(F32)), flux_turned[...])
        scaled = (spread[:slots] + spread[slots:]) * speeds
        summed = nn(gather_rows, two_terms(scaled))
        return vector + lift_and_precondition(summed)

    first_vec = operate(0, start_vec)
    vec_out[1] = packed(first_vec)
    send_vector(1)
    lane_ids = lax.broadcasted_iota(jnp.int32, (1, LANES), 1)

    def total_at(lane, x):
        column = jnp.sum(x, axis=1, keepdims=True)
        return jnp.where(lane_ids == lane, jnp.sum(column, axis=0, keepdims=True), 0.0)

    early = total_at(0, first_vec * first_vec) + total_at(3, start_vec * first_vec)
    second_vec = operate(1, first_vec)

    partial = (
        early
        + total_at(1, first_vec * second_vec)
        + total_at(2, second_vec * second_vec)
        + total_at(4, start_vec * second_vec)
    )
    base = 0
    for index, peers in enumerate(stages):
        sums_out[index] = partial
        for j, peer in enumerate(peers):
            pltpu.make_async_remote_copy(
                sums_out.at[index],
                sums_in.at[base + j],
                sums_send.at[index],
                sums_recv.at[index],
                peer,
                MESH,
            ).start()
        landed = sums_in.at[pl.ds(base, len(peers))]
        await_recv(landed, sums_send.at[index], sums_recv.at[index], (ahead, f))
        partial += jnp.sum(sums_in[base : base + len(peers)], axis=0)
        base += len(peers)

    norm_first = partial[:, 0:1]
    cross_term = partial[:, 1:2]
    norm_second = partial[:, 2:3]
    proj_first = partial[:, 3:4]
    proj_second = partial[:, 4:5]
    ridge = 0.001 * (norm_first + norm_second)
    determinant = (norm_first + ridge) * (norm_second + ridge) - cross_term * cross_term
    coef_first = (proj_first * (norm_second + ridge) - proj_second * cross_term) / determinant
    coef_second = (proj_second * (norm_first + ridge) - proj_first * cross_term) / determinant
    terms_ref[0] = coef_first * start_vec
    terms_ref[1] = coef_second * first_vec
    terms_ref[2] = start_vec - coef_first * first_vec
    terms_ref[3] = coef_second * second_vec

    send_meta.wait_send()
    send_metric.wait_send()
    await_send(state_in, setup_send.at[2], setup_recv.at[2], (ahead, f))
    for step in range(2):
        await_send(vec_in.at[step], vec_send.at[step], vec_recv.at[step], (ahead, f))
    base = 0
    for index, peers in enumerate(stages):
        landed = sums_in.at[pl.ds(base, len(peers))]
        await_send(landed, sums_send.at[index], sums_recv.at[index], (ahead, f))
        base += len(peers)


def on_device(
    n_dom,
    n_face,
    elem_state,
    face_metric,
    right_side,
    block_inverse,
    trace_basis,
    flux_basis,
    face_rows,
    face_cols,
    face_counts,
):
    own, nv = right_side.shape
    slots = face_rows.shape[0]
    radices = radices_of(n_dom)
    exchanges = n_face - 1 + sum(r - 1 for r in radices)
    dma = pltpu.SemaphoreType.DMA
    vmem = pl.BlockSpec(memory_space=pltpu.VMEM)
    hbm = pl.BlockSpec(memory_space=pltpu.HBM)
    terms = pl.pallas_call(
        functools.partial(kernel, n_dom, n_face),
        out_shape=pltpu.VMEM((4, own, nv), F32),
        in_specs=[hbm] * 9,
        out_specs=vmem,
        scratch_shapes=[
            pltpu.VMEM((own, nv), BF16),
            pltpu.VMEM((own, nv), F32),
            pltpu.VMEM((own, nv, nv), BF16),
            pltpu.VMEM((own, nv, nv), BF16),
            pltpu.VMEM((nv, nv), BF16),
            pltpu.VMEM((nv, nv), BF16),
            pltpu.VMEM((nv, nv), BF16),
            pltpu.VMEM((nv, nv), BF16),
            pltpu.VMEM((1, slots), jnp.int32),
            pltpu.VMEM((1, slots), jnp.int32),
            pltpu.VMEM((1, 1), jnp.int32),
            pltpu.VMEM((2 * own, PART), BF16),
            pltpu.VMEM((n_face, 2 * own, PART), BF16),
            pltpu.VMEM((8, LANES), jnp.int32),
            pltpu.VMEM((8, LANES), jnp.int32),
            pltpu.VMEM((slots, nv), BF16),
            pltpu.VMEM((2, 2 * own, PART), BF16),
            pltpu.VMEM((2, n_face, 2 * own, PART), BF16),
            pltpu.VMEM((1 + len(radices), 1, LANES), F32),
            pltpu.VMEM((exchanges, 1, LANES), F32),
            dma((own + 7,)),
            dma((3,)),
            dma((3,)),
            dma((2,)),
            dma((2,)),
            dma((1 + len(radices),)),
            dma((1 + len(radices),)),
        ],
        compiler_params=pltpu.CompilerParams(
            collective_id=0, has_side_effects=True, vmem_limit_bytes=24 * 1024 * 1024
        ),
    )(
        *(
            pltpu.with_memory_space_constraint(operand, pltpu.HBM)
            for operand in (
                elem_state,
                face_metric,
                right_side,
                block_inverse,
                trace_basis,
                flux_basis,
                face_rows.reshape(1, slots),
                face_cols.reshape(1, slots),
            )
        ),
        face_counts.reshape(1, 1),
    )
    return terms[0] + terms[1], terms[2] - terms[3]


def solution(mesh):
    split = P(("dom", "face"))
    return jax.shard_map(
        functools.partial(on_device, mesh.shape["dom"], mesh.shape["face"]),
        mesh=mesh,
        in_specs=(
            P(("dom", "face"), None),
            P(("dom", "face"), None),
            P(("dom", "face"), None),
            P(("dom", "face"), None, None),
            P(),
            P(),
            split,
            split,
            split,
        ),
        out_specs=(P(("dom", "face"), None), P(("dom", "face"), None)),
        check_vma=False,
    )
```

```python
import functools

import jax
import jax.numpy as jnp
from jax import lax
from jax.experimental import pallas as pl
from jax.experimental.pallas import tpu as pltpu
from jax.sharding import PartitionSpec as P

MESH = pl.DeviceIdType.MESH
F32 = jnp.float32
BF16 = jnp.bfloat16
LANES = 128
MAX_RADIX = 8
PART = 256


def radices_of(count):
    radices = []
    while count > 1:
        best = next((r for r in range(MAX_RADIX, 1, -1) if count % r == 0), None)
        if best is None:
            best = next(r for r in range(MAX_RADIX + 1, count + 1) if count % r == 0)
        radices.append(best)
        count //= best
    return radices


def nn(a, b):
    return jnp.dot(a, b, preferred_element_type=F32)


def nt(a, b):
    return lax.dot_general(a, b, (((1,), (1,)), ((), ())), preferred_element_type=F32)


def two_terms(x):
    high = x.astype(BF16).astype(F32)
    return jnp.concatenate([high, x - high], axis=0).astype(BF16)


def packed(x):
    right = x[:, PART:]
    right = jnp.concatenate([right, jnp.zeros((x.shape[0], 2 * PART - x.shape[1]), F32)], axis=1)
    return jnp.concatenate([x[:, :PART], right], axis=0).astype(BF16)


def await_recv(ref, send_sem, recv_sem, peer):
    pltpu.make_async_remote_copy(ref, ref, send_sem, recv_sem, peer, MESH).wait_recv()


def await_send(ref, send_sem, recv_sem, peer):
    pltpu.make_async_remote_copy(ref, ref, send_sem, recv_sem, peer, MESH).wait_send()


def kernel(
    n_dom,
    n_face,
    state_hbm,
    metric_hbm,
    rhs_hbm,
    binv_hbm,
    trace_hbm,
    flux_hbm,
    rows_hbm,
    cols_hbm,
    count_hbm,
    terms_ref,
    state,
    rhs,
    binv,
    solved,
    trace,
    trace_turned,
    flux,
    flux_turned,
    rows,
    cols,
    count,
    state_out,
    state_in,
    meta_out,
    meta_in,
    metric_in,
    vec_out,
    vec_in,
    sums_out,
    sums_in,
    load_sem,
    setup_send,
    setup_recv,
    vec_send,
    vec_recv,
    sums_send,
    sums_recv,
):
    d = lax.axis_index("dom")
    f = lax.axis_index("face")
    ahead = lax.rem(d + 1, n_dom)
    behind = lax.rem(d + n_dom - 1, n_dom)
    own, nv = rhs.shape
    slots = metric_in.shape[0]

    small = [
        pltpu.make_async_copy(src, dst, load_sem.at[own + at])
        for at, (src, dst) in enumerate(
            (
                (rhs_hbm, rhs),
                (cols_hbm, cols),
                (rows_hbm, rows),
                (count_hbm, count),
                (state_hbm, state),
                (trace_hbm, trace),
                (flux_hbm, flux),
            )
        )
    ]
    loads = [
        pltpu.make_async_copy(binv_hbm.at[e], binv.at[e], load_sem.at[e]) for e in range(own)
    ]
    for load in small[:5] + loads + small[5:]:
        load.start()

    radices = radices_of(n_dom)
    low = lax.rem(d, radices[0])
    group = n_face * radices[0]
    flat = low * n_face + f
    stages = []
    peers = []
    for j in range(1, group):
        other = lax.rem(flat + j, group)
        peers.append((d - low + other // n_face, lax.rem(other, n_face)))
    stages.append(peers)
    stride = radices[0]
    for radix in radices[1:]:
        digit = lax.rem(d // stride, radix)
        stages.append(
            [(d + (lax.rem(digit + j, radix) - digit) * stride, f) for j in range(1, radix)]
        )
        stride *= radix

    barrier = pltpu.get_barrier_semaphore()
    greeted = 0
    greet = [peer for peers in stages for peer in peers]
    if len(radices) > 1:
        greet += [(dom, peer) for peer in range(n_face) for dom in (ahead, behind)]
    for peer in greet:
        pl.semaphore_signal(barrier, inc=1, device_id=peer, device_id_type=MESH)
        greeted += 1

    row_ids = lax.broadcasted_iota(jnp.int32, (own, nv), 0)

    def precondition(vector):
        rounded = vector.astype(BF16).astype(F32)
        total = jnp.zeros((own, nv), F32)
        for e in range(own):
            loads[e].wait()
            total += nt(jnp.where(row_ids == e, rounded, 0.0).astype(BF16), binv[e])
        return total

    def lift_and_precondition(vector):
        high = vector.astype(BF16).astype(F32)
        terms = jnp.concatenate([high, vector - high], axis=0)
        term_ids = jnp.concatenate([row_ids, row_ids], axis=0)
        total = jnp.zeros((2 * own, nv), F32)
        for e in range(own):
            total += nn(jnp.where(term_ids == e, terms, 0.0).astype(BF16), solved[e])
        return total[:own] + total[own:]

    def send_vector(step):
        for peer in range(n_face):
            pltpu.make_async_remote_copy(
                vec_out.at[step],
                vec_in.at[step, f],
                vec_send.at[step],
                vec_recv.at[step],
                (ahead, peer),
                MESH,
            ).start()

    small[1].wait()
    small[2].wait()
    small[3].wait()
    small[4].wait()
    slot_ids = lax.broadcasted_iota(jnp.int32, (1, slots), 1)
    meta_out[...] = jnp.zeros_like(meta_out)
    meta_out[0:1, 0:slots] = jnp.where(slot_ids < count[...], cols[...], -1)
    meta_out[1:2, 0:slots] = rows[...]
    state_out[...] = packed(state[...].astype(F32))
    small[0].wait()
    start_vec = precondition(rhs[...])
    vec_out[0] = packed(start_vec)

    pl.semaphore_wait(barrier, greeted)

    send_vector(0)
    send_meta = pltpu.make_async_remote_copy(
        meta_out, meta_in, setup_send.at[0], setup_recv.at[0], (ahead, f), MESH
    )
    send_meta.start()
    for peer in range(n_face):
        pltpu.make_async_remote_copy(
            state_out, state_in.at[f], setup_send.at[2], setup_recv.at[2], (ahead, peer), MESH
        ).start()
    send_metric = pltpu.make_async_remote_copy(
        metric_hbm, metric_in, setup_send.at[1], setup_recv.at[1], (ahead, f), MESH
    )
    send_metric.start()

    small[5].wait()
    small[6].wait()
    flux_turned[...] = flux[...].T
    trace_turned[...] = trace[...].T
    for e in range(own):
        solved[e] = nt(trace_turned[...], binv[e]).astype(BF16)

    send_meta.wait_recv()
    own_ids = lax.broadcasted_iota(jnp.int32, (own, slots), 0)
    absent = jnp.full((own, slots), -2, jnp.int32)
    left_ids, right_ids = [], []
    for peer in range(n_face):
        left_ids += [own_ids + peer * own, absent]
        right_ids += [absent, own_ids + peer * own]
    slot_cols = meta_in[0:1, 0:slots]
    pick_left = (jnp.concatenate(left_ids, axis=0) == slot_cols).astype(F32)
    pick_right = (jnp.concatenate(right_ids, axis=0) == slot_cols).astype(F32)
    pick = jnp.concatenate([pick_left, pick_right], axis=1).T.astype(BF16)
    gather_rows = (own_ids == meta_in[1:2, 0:slots]).astype(F32)
    gather_rows = jnp.concatenate([gather_rows, gather_rows], axis=1).astype(BF16)

    def picked(blocks):
        both = nn(pick, blocks.reshape(n_face * 2 * own, PART))
        return both[:slots], both[slots:, : nv - PART]

    await_recv(state_in, setup_send.at[2], setup_recv.at[2], (ahead, f))
    speeds = 1.0 + 0.5 * jnp.tanh(jnp.concatenate(picked(state_in[...]), axis=1))
    send_metric.wait_recv()

    def operate(step, vector):
        await_recv(vec_in.at[step], vec_send.at[step], vec_recv.at[step], (ahead, f))
        left, right = picked(vec_in[step])
        lifted = nn(left.astype(BF16), trace[0:PART]) + nn(right.astype(BF16), trace[PART:nv])
        spread = nn(two_terms(lifted * metric_in[...].astype(F32)), flux_turned[...])
        scaled = (spread[:slots] + spread[slots:]) * speeds
        summed = nn(gather_rows, two_terms(scaled))
        return vector + lift_and_precondition(summed)

    first_vec = operate(0, start_vec)
    vec_out[1] = packed(first_vec)
    send_vector(1)
    lane_ids = lax.broadcasted_iota(jnp.int32, (1, LANES), 1)

    def total_at(lane, x):
        column = jnp.sum(x, axis=1, keepdims=True)
        return jnp.where(lane_ids == lane, jnp.sum(column, axis=0, keepdims=True), 0.0)

    early = total_at(0, first_vec * first_vec) + total_at(3, start_vec * first_vec)
    second_vec = operate(1, first_vec)

    partial = (
        early
        + total_at(1, first_vec * second_vec)
        + total_at(2, second_vec * second_vec)
        + total_at(4, start_vec * second_vec)
    )
    base = 0
    for index, peers in enumerate(stages):
        sums_out[index] = partial
        for j, peer in enumerate(peers):
            pltpu.make_async_remote_copy(
                sums_out.at[index],
                sums_in.at[base + j],
                sums_send.at[index],
                sums_recv.at[index],
                peer,
                MESH,
            ).start()
        landed = sums_in.at[pl.ds(base, len(peers))]
        await_recv(landed, sums_send.at[index], sums_recv.at[index], (ahead, f))
        partial += jnp.sum(sums_in[base : base + len(peers)], axis=0)
        base += len(peers)

    norm_first = partial[:, 0:1]
    cross_term = partial[:, 1:2]
    norm_second = partial[:, 2:3]
    proj_first = partial[:, 3:4]
    proj_second = partial[:, 4:5]
    ridge = 0.001 * (norm_first + norm_second)
    determinant = (norm_first + ridge) * (norm_second + ridge) - cross_term * cross_term
    coef_first = (proj_first * (norm_second + ridge) - proj_second * cross_term) / determinant
    coef_second = (proj_second * (norm_first + ridge) - proj_first * cross_term) / determinant
    terms_ref[0] = coef_first * start_vec
    terms_ref[1] = coef_second * first_vec
    terms_ref[2] = start_vec - coef_first * first_vec
    terms_ref[3] = coef_second * second_vec

    send_meta.wait_send()
    send_metric.wait_send()
    await_send(state_in, setup_send.at[2], setup_recv.at[2], (ahead, f))
    for step in range(2):
        await_send(vec_in.at[step], vec_send.at[step], vec_recv.at[step], (ahead, f))
    base = 0
    for index, peers in enumerate(stages):
        landed = sums_in.at[pl.ds(base, len(peers))]
        await_send(landed, sums_send.at[index], sums_recv.at[index], (ahead, f))
        base += len(peers)


def on_device(
    n_dom,
    n_face,
    elem_state,
    face_metric,
    right_side,
    block_inverse,
    trace_basis,
    flux_basis,
    face_rows,
    face_cols,
    face_counts,
):
    own, nv = right_side.shape
    slots = face_rows.shape[0]
    radices = radices_of(n_dom)
    exchanges = n_face * radices[0] - 1 + sum(r - 1 for r in radices[1:])
    dma = pltpu.SemaphoreType.DMA
    vmem = pl.BlockSpec(memory_space=pltpu.VMEM)
    hbm = pl.BlockSpec(memory_space=pltpu.HBM)
    terms = pl.pallas_call(
        functools.partial(kernel, n_dom, n_face),
        out_shape=pltpu.VMEM((4, own, nv), F32),
        in_specs=[hbm] * 9,
        out_specs=vmem,
        scratch_shapes=[
            pltpu.VMEM((own, nv), BF16),
            pltpu.VMEM((own, nv), F32),
            pltpu.VMEM((own, nv, nv), BF16),
            pltpu.VMEM((own, nv, nv), BF16),
            pltpu.VMEM((nv, nv), BF16),
            pltpu.VMEM((nv, nv), BF16),
            pltpu.VMEM((nv, nv), BF16),
            pltpu.VMEM((nv, nv), BF16),
            pltpu.VMEM((1, slots), jnp.int32),
            pltpu.VMEM((1, slots), jnp.int32),
            pltpu.VMEM((1, 1), jnp.int32),
            pltpu.VMEM((2 * own, PART), BF16),
            pltpu.VMEM((n_face, 2 * own, PART), BF16),
            pltpu.VMEM((8, LANES), jnp.int32),
            pltpu.VMEM((8, LANES), jnp.int32),
            pltpu.VMEM((slots, nv), BF16),
            pltpu.VMEM((2, 2 * own, PART), BF16),
            pltpu.VMEM((2, n_face, 2 * own, PART), BF16),
            pltpu.VMEM((len(radices), 1, LANES), F32),
            pltpu.VMEM((exchanges, 1, LANES), F32),
            dma((own + 7,)),
            dma((3,)),
            dma((3,)),
            dma((2,)),
            dma((2,)),
            dma((len(radices),)),
            dma((len(radices),)),
        ],
        compiler_params=pltpu.CompilerParams(
            collective_id=0, has_side_effects=True, vmem_limit_bytes=24 * 1024 * 1024
        ),
    )(
        *(
            pltpu.with_memory_space_constraint(operand, pltpu.HBM)
            for operand in (
                elem_state,
                face_metric,
                right_side,
                block_inverse,
                trace_basis,
                flux_basis,
                face_rows.reshape(1, slots),
                face_cols.reshape(1, slots),
            )
        ),
        face_counts.reshape(1, 1),
    )
    return terms[0] + terms[1], terms[2] - terms[3]


def solution(mesh):
    split = P(("dom", "face"))
    return jax.shard_map(
        functools.partial(on_device, mesh.shape["dom"], mesh.shape["face"]),
        mesh=mesh,
        in_specs=(
            P(("dom", "face"), None),
            P(("dom", "face"), None),
            P(("dom", "face"), None),
            P(("dom", "face"), None, None),
            P(),
            P(),
            split,
            split,
            split,
        ),
        out_specs=(P(("dom", "face"), None), P(("dom", "face"), None)),
        check_vma=False,
    )
```

```python
import functools

import jax
import jax.numpy as jnp
from jax import lax
from jax.experimental import pallas as pl
from jax.experimental.pallas import tpu as pltpu
from jax.sharding import PartitionSpec as P

MESH = pl.DeviceIdType.MESH
F32 = jnp.float32
BF16 = jnp.bfloat16
LANES = 128
MAX_RADIX = 8
PART = 256


def radices_of(count):
    radices = []
    while count > 1:
        best = next((r for r in range(MAX_RADIX, 1, -1) if count % r == 0), None)
        if best is None:
            best = next(r for r in range(MAX_RADIX + 1, count + 1) if count % r == 0)
        radices.append(best)
        count //= best
    return radices


def nn(a, b):
    return jnp.dot(a, b, preferred_element_type=F32)


def nt(a, b):
    return lax.dot_general(a, b, (((1,), (1,)), ((), ())), preferred_element_type=F32)


def two_terms(x):
    high = x.astype(BF16).astype(F32)
    return jnp.concatenate([high, x - high], axis=0).astype(BF16)


def packed(x):
    right = x[:, PART:]
    right = jnp.concatenate([right, jnp.zeros((x.shape[0], 2 * PART - x.shape[1]), F32)], axis=1)
    return jnp.concatenate([x[:, :PART], right], axis=0).astype(BF16)


def await_recv(ref, send_sem, recv_sem, peer):
    pltpu.make_async_remote_copy(ref, ref, send_sem, recv_sem, peer, MESH).wait_recv()


def await_send(ref, send_sem, recv_sem, peer):
    pltpu.make_async_remote_copy(ref, ref, send_sem, recv_sem, peer, MESH).wait_send()


def kernel(
    n_dom,
    n_face,
    state_hbm,
    metric_hbm,
    rhs_hbm,
    binv_hbm,
    trace_hbm,
    flux_hbm,
    rows_hbm,
    cols_hbm,
    count_hbm,
    terms_ref,
    state,
    rhs,
    binv,
    trace,
    trace_turned,
    flux,
    flux_turned,
    rows,
    cols,
    count,
    state_out,
    state_in,
    meta_out,
    meta_in,
    metric_in,
    vec_out,
    vec_in,
    sums_out,
    sums_in,
    load_sem,
    setup_send,
    setup_recv,
    vec_send,
    vec_recv,
    sums_send,
    sums_recv,
):
    d = lax.axis_index("dom")
    f = lax.axis_index("face")
    ahead = lax.rem(d + 1, n_dom)
    behind = lax.rem(d + n_dom - 1, n_dom)
    own, nv = rhs.shape
    slots = metric_in.shape[0]

    small = [
        pltpu.make_async_copy(src, dst, load_sem.at[own + at])
        for at, (src, dst) in enumerate(
            (
                (rhs_hbm, rhs),
                (cols_hbm, cols),
                (rows_hbm, rows),
                (count_hbm, count),
                (state_hbm, state),
                (trace_hbm, trace),
                (flux_hbm, flux),
            )
        )
    ]
    loads = [
        pltpu.make_async_copy(binv_hbm.at[e], binv.at[e], load_sem.at[e]) for e in range(own)
    ]
    for load in small[:5] + loads + small[5:]:
        load.start()

    radices = radices_of(n_dom)
    low = lax.rem(d, radices[0])
    group = n_face * radices[0]
    flat = low * n_face + f
    stages = []
    peers = []
    for j in range(1, group):
        other = lax.rem(flat + j, group)
        peers.append((d - low + other // n_face, lax.rem(other, n_face)))
    stages.append(peers)
    stride = radices[0]
    for radix in radices[1:]:
        digit = lax.rem(d // stride, radix)
        stages.append(
            [(d + (lax.rem(digit + j, radix) - digit) * stride, f) for j in range(1, radix)]
        )
        stride *= radix

    barrier = pltpu.get_barrier_semaphore()
    greeted = 0
    greet = [peer for peers in stages for peer in peers]
    if len(radices) > 1:
        greet += [(dom, peer) for peer in range(n_face) for dom in (ahead, behind)]
    for peer in greet:
        pl.semaphore_signal(barrier, inc=1, device_id=peer, device_id_type=MESH)
        greeted += 1

    row_ids = lax.broadcasted_iota(jnp.int32, (own, nv), 0)

    def precondition(vector):
        rounded = vector.astype(BF16).astype(F32)
        total = jnp.zeros((own, nv), F32)
        for e in range(own):
            total += nt(jnp.where(row_ids == e, rounded, 0.0).astype(BF16), binv[e])
        return total

    def send_vector(step):
        for peer in range(n_face):
            pltpu.make_async_remote_copy(
                vec_out.at[step],
                vec_in.at[step, f],
                vec_send.at[step],
                vec_recv.at[step],
                (ahead, peer),
                MESH,
            ).start()

    small[1].wait()
    small[2].wait()
    small[3].wait()
    small[4].wait()
    slot_ids = lax.broadcasted_iota(jnp.int32, (1, slots), 1)
    meta_out[...] = jnp.zeros_like(meta_out)
    meta_out[0:1, 0:slots] = jnp.where(slot_ids < count[...], cols[...], -1)
    meta_out[1:2, 0:slots] = rows[...]
    state_out[...] = packed(state[...].astype(F32))

    pl.semaphore_wait(barrier, greeted)

    send_meta = pltpu.make_async_remote_copy(
        meta_out, meta_in, setup_send.at[0], setup_recv.at[0], (ahead, f), MESH
    )
    send_meta.start()
    for peer in range(n_face):
        pltpu.make_async_remote_copy(
            state_out, state_in.at[f], setup_send.at[2], setup_recv.at[2], (ahead, peer), MESH
        ).start()
    send_metric = pltpu.make_async_remote_copy(
        metric_hbm, metric_in, setup_send.at[1], setup_recv.at[1], (ahead, f), MESH
    )
    send_metric.start()

    small[0].wait()
    for load in loads:
        load.wait()
    start_vec = precondition(rhs[...])
    vec_out[0] = packed(start_vec)
    send_vector(0)

    small[5].wait()
    small[6].wait()
    flux_turned[...] = flux[...].T
    trace_turned[...] = trace[...].T

    send_meta.wait_recv()
    own_ids = lax.broadcasted_iota(jnp.int32, (own, slots), 0)
    absent = jnp.full((own, slots), -2, jnp.int32)
    left_ids, right_ids = [], []
    for peer in range(n_face):
        left_ids += [own_ids + peer * own, absent]
        right_ids += [absent, own_ids + peer * own]
    slot_cols = meta_in[0:1, 0:slots]
    pick_left = (jnp.concatenate(left_ids, axis=0) == slot_cols).astype(F32)
    pick_right = (jnp.concatenate(right_ids, axis=0) == slot_cols).astype(F32)
    pick = jnp.concatenate([pick_left, pick_right], axis=1).T.astype(BF16)
    gather_rows = (own_ids == meta_in[1:2, 0:slots]).astype(F32)
    gather_rows = jnp.concatenate([gather_rows, gather_rows], axis=1).astype(BF16)

    def picked(blocks):
        both = nn(pick, blocks.reshape(n_face * 2 * own, PART))
        return both[:slots], both[slots:, : nv - PART]

    await_recv(state_in, setup_send.at[2], setup_recv.at[2], (ahead, f))
    speeds = 1.0 + 0.5 * jnp.tanh(jnp.concatenate(picked(state_in[...]), axis=1))
    send_metric.wait_recv()

    def operate(step, vector):
        await_recv(vec_in.at[step], vec_send.at[step], vec_recv.at[step], (ahead, f))
        left, right = picked(vec_in[step])
        lifted = nn(left.astype(BF16), trace[0:PART]) + nn(right.astype(BF16), trace[PART:nv])
        spread = nn(two_terms(lifted * metric_in[...].astype(F32)), flux_turned[...])
        scaled = (spread[:slots] + spread[slots:]) * speeds
        summed = nn(gather_rows, two_terms(scaled))
        back = nn(two_terms(summed), trace_turned[...])
        return vector + precondition(back[:own] + back[own:])

    first_vec = operate(0, start_vec)
    vec_out[1] = packed(first_vec)
    send_vector(1)
    lane_ids = lax.broadcasted_iota(jnp.int32, (1, LANES), 1)

    def total_at(lane, x):
        column = jnp.sum(x, axis=1, keepdims=True)
        return jnp.where(lane_ids == lane, jnp.sum(column, axis=0, keepdims=True), 0.0)

    early = total_at(0, first_vec * first_vec) + total_at(3, start_vec * first_vec)
    second_vec = operate(1, first_vec)

    partial = (
        early
        + total_at(1, first_vec * second_vec)
        + total_at(2, second_vec * second_vec)
        + total_at(4, start_vec * second_vec)
    )
    base = 0
    for index, peers in enumerate(stages):
        sums_out[index] = partial
        for j, peer in enumerate(peers):
            pltpu.make_async_remote_copy(
                sums_out.at[index],
                sums_in.at[base + j],
                sums_send.at[index],
                sums_recv.at[index],
                peer,
                MESH,
            ).start()
        landed = sums_in.at[pl.ds(base, len(peers))]
        await_recv(landed, sums_send.at[index], sums_recv.at[index], (ahead, f))
        partial += jnp.sum(sums_in[base : base + len(peers)], axis=0)
        base += len(peers)

    norm_first = partial[:, 0:1]
    cross_term = partial[:, 1:2]
    norm_second = partial[:, 2:3]
    proj_first = partial[:, 3:4]
    proj_second = partial[:, 4:5]
    ridge = 0.001 * (norm_first + norm_second)
    determinant = (norm_first + ridge) * (norm_second + ridge) - cross_term * cross_term
    coef_first = (proj_first * (norm_second + ridge) - proj_second * cross_term) / determinant
    coef_second = (proj_second * (norm_first + ridge) - proj_first * cross_term) / determinant
    terms_ref[0] = coef_first * start_vec
    terms_ref[1] = coef_second * first_vec
    terms_ref[2] = start_vec - coef_first * first_vec
    terms_ref[3] = coef_second * second_vec

    send_meta.wait_send()
    send_metric.wait_send()
    await_send(state_in, setup_send.at[2], setup_recv.at[2], (ahead, f))
    for step in range(2):
        await_send(vec_in.at[step], vec_send.at[step], vec_recv.at[step], (ahead, f))
    base = 0
    for index, peers in enumerate(stages):
        landed = sums_in.at[pl.ds(base, len(peers))]
        await_send(landed, sums_send.at[index], sums_recv.at[index], (ahead, f))
        base += len(peers)


def on_device(
    n_dom,
    n_face,
    elem_state,
    face_metric,
    right_side,
    block_inverse,
    trace_basis,
    flux_basis,
    face_rows,
    face_cols,
    face_counts,
):
    own, nv = right_side.shape
    slots = face_rows.shape[0]
    radices = radices_of(n_dom)
    exchanges = n_face * radices[0] - 1 + sum(r - 1 for r in radices[1:])
    dma = pltpu.SemaphoreType.DMA
    vmem = pl.BlockSpec(memory_space=pltpu.VMEM)
    hbm = pl.BlockSpec(memory_space=pltpu.HBM)
    terms = pl.pallas_call(
        functools.partial(kernel, n_dom, n_face),
        out_shape=pltpu.VMEM((4, own, nv), F32),
        in_specs=[hbm] * 9,
        out_specs=vmem,
        scratch_shapes=[
            pltpu.VMEM((own, nv), BF16),
            pltpu.VMEM((own, nv), F32),
            pltpu.VMEM((own, nv, nv), BF16),
            pltpu.VMEM((nv, nv), BF16),
            pltpu.VMEM((nv, nv), BF16),
            pltpu.VMEM((nv, nv), BF16),
            pltpu.VMEM((nv, nv), BF16),
            pltpu.VMEM((1, slots), jnp.int32),
            pltpu.VMEM((1, slots), jnp.int32),
            pltpu.VMEM((1, 1), jnp.int32),
            pltpu.VMEM((2 * own, PART), BF16),
            pltpu.VMEM((n_face, 2 * own, PART), BF16),
            pltpu.VMEM((8, LANES), jnp.int32),
            pltpu.VMEM((8, LANES), jnp.int32),
            pltpu.VMEM((slots, nv), BF16),
            pltpu.VMEM((2, 2 * own, PART), BF16),
            pltpu.VMEM((2, n_face, 2 * own, PART), BF16),
            pltpu.VMEM((len(radices), 1, LANES), F32),
            pltpu.VMEM((exchanges, 1, LANES), F32),
            dma((own + 7,)),
            dma((3,)),
            dma((3,)),
            dma((2,)),
            dma((2,)),
            dma((len(radices),)),
            dma((len(radices),)),
        ],
        compiler_params=pltpu.CompilerParams(
            collective_id=0, has_side_effects=True, vmem_limit_bytes=24 * 1024 * 1024
        ),
    )(
        *(
            pltpu.with_memory_space_constraint(operand, pltpu.HBM)
            for operand in (
                elem_state,
                face_metric,
                right_side,
                block_inverse,
                trace_basis,
                flux_basis,
                face_rows.reshape(1, slots),
                face_cols.reshape(1, slots),
            )
        ),
        face_counts.reshape(1, 1),
    )
    return terms[0] + terms[1], terms[2] - terms[3]


def solution(mesh):
    split = P(("dom", "face"))
    return jax.shard_map(
        functools.partial(on_device, mesh.shape["dom"], mesh.shape["face"]),
        mesh=mesh,
        in_specs=(
            P(("dom", "face"), None),
            P(("dom", "face"), None),
            P(("dom", "face"), None),
            P(("dom", "face"), None, None),
            P(),
            P(),
            split,
            split,
            split,
        ),
        out_specs=(P(("dom", "face"), None), P(("dom", "face"), None)),
        check_vma=False,
    )
```

```python
import functools

import jax
import jax.numpy as jnp
from jax import lax
from jax.experimental import pallas as pl
from jax.experimental.pallas import tpu as pltpu
from jax.sharding import PartitionSpec as P

MESH = pl.DeviceIdType.MESH
F32 = jnp.float32
BF16 = jnp.bfloat16
LANES = 128
MAX_RADIX = 8


def radices_of(count):
    radices = []
    while count > 1:
        best = next((r for r in range(MAX_RADIX, 1, -1) if count % r == 0), None)
        if best is None:
            best = next(r for r in range(MAX_RADIX + 1, count + 1) if count % r == 0)
        radices.append(best)
        count //= best
    return radices


def nn(a, b):
    return jnp.dot(a, b, preferred_element_type=F32)


def nt(a, b):
    return lax.dot_general(a, b, (((1,), (1,)), ((), ())), preferred_element_type=F32)


def two_terms(x):
    high = x.astype(BF16).astype(F32)
    return jnp.concatenate([high, x - high], axis=0).astype(BF16)


def await_recv(ref, send_sem, recv_sem, peer):
    pltpu.make_async_remote_copy(ref, ref, send_sem, recv_sem, peer, MESH).wait_recv()


def await_send(ref, send_sem, recv_sem, peer):
    pltpu.make_async_remote_copy(ref, ref, send_sem, recv_sem, peer, MESH).wait_send()


def kernel(
    n_dom,
    n_face,
    state_hbm,
    metric_hbm,
    rhs_hbm,
    binv_hbm,
    trace_hbm,
    flux_hbm,
    rows_hbm,
    cols_hbm,
    count_hbm,
    terms_ref,
    state,
    rhs,
    binv,
    solved,
    trace,
    trace_turned,
    flux,
    flux_turned,
    rows,
    cols,
    count,
    state_in,
    meta_out,
    meta_in,
    metric_in,
    vec_out,
    vec_in,
    sums_out,
    sums_in,
    load_sem,
    setup_send,
    setup_recv,
    vec_send,
    vec_recv,
    sums_send,
    sums_recv,
):
    d = lax.axis_index("dom")
    f = lax.axis_index("face")
    ahead = lax.rem(d + 1, n_dom)
    behind = lax.rem(d + n_dom - 1, n_dom)
    own, nv = rhs.shape
    slots = metric_in.shape[0]

    small = [
        pltpu.make_async_copy(src, dst, load_sem.at[own + at])
        for at, (src, dst) in enumerate(
            (
                (rhs_hbm, rhs),
                (cols_hbm, cols),
                (rows_hbm, rows),
                (count_hbm, count),
                (state_hbm, state),
                (trace_hbm, trace),
                (flux_hbm, flux),
            )
        )
    ]
    loads = [
        pltpu.make_async_copy(binv_hbm.at[e], binv.at[e], load_sem.at[e]) for e in range(own)
    ]
    for load in small[:5] + loads + small[5:]:
        load.start()

    radices = radices_of(n_dom)
    low = lax.rem(d, radices[0])
    group = n_face * radices[0]
    flat = low * n_face + f
    stages = []
    peers = []
    for j in range(group - 1, 0, -1):
        other = lax.rem(flat + j, group)
        peers.append((d - low + other // n_face, lax.rem(other, n_face)))
    stages.append(peers)
    stride = radices[0]
    for radix in radices[1:]:
        digit = lax.rem(d // stride, radix)
        stages.append(
            [(d + (lax.rem(digit + j, radix) - digit) * stride, f) for j in range(1, radix)]
        )
        stride *= radix

    barrier = pltpu.get_barrier_semaphore()
    greeted = 0
    greet = [peer for peers in stages for peer in peers]
    if len(radices) > 1:
        greet += [(dom, peer) for peer in range(n_face) for dom in (ahead, behind)]
    for peer in greet:
        pl.semaphore_signal(barrier, inc=1, device_id=peer, device_id_type=MESH)
        greeted += 1

    row_ids = lax.broadcasted_iota(jnp.int32, (own, nv), 0)

    def precondition(vector):
        rounded = vector.astype(BF16).astype(F32)
        total = jnp.zeros((own, nv), F32)
        for e in range(own):
            loads[e].wait()
            total += nt(jnp.where(row_ids == e, rounded, 0.0).astype(BF16), binv[e])
        return total

    def lift_and_precondition(vector):
        high = vector.astype(BF16).astype(F32)
        terms = jnp.concatenate([high, vector - high], axis=0)
        term_ids = jnp.concatenate([row_ids, row_ids], axis=0)
        total = jnp.zeros((2 * own, nv), F32)
        for e in range(own):
            total += nn(jnp.where(term_ids == e, terms, 0.0).astype(BF16), solved[e])
        return total[:own] + total[own:]

    def send_vector(step):
        for peer in range(n_face):
            pltpu.make_async_remote_copy(
                vec_out.at[step],
                vec_in.at[step, f],
                vec_send.at[step],
                vec_recv.at[step],
                (ahead, peer),
                MESH,
            ).start()

    small[1].wait()
    small[2].wait()
    small[3].wait()
    small[4].wait()
    slot_ids = lax.broadcasted_iota(jnp.int32, (1, slots), 1)
    meta_out[...] = jnp.zeros_like(meta_out)
    meta_out[0:1, 0:slots] = jnp.where(slot_ids < count[...], cols[...], -1)
    meta_out[1:2, 0:slots] = rows[...]

    pl.semaphore_wait(barrier, greeted)

    send_meta = pltpu.make_async_remote_copy(
        meta_out, meta_in, setup_send.at[0], setup_recv.at[0], (ahead, f), MESH
    )
    send_meta.start()
    for peer in range(n_face):
        pltpu.make_async_remote_copy(
            state, state_in.at[f], setup_send.at[2], setup_recv.at[2], (ahead, peer), MESH
        ).start()
    send_metric = pltpu.make_async_remote_copy(
        metric_hbm, metric_in, setup_send.at[1], setup_recv.at[1], (ahead, f), MESH
    )
    send_metric.start()

    small[0].wait()
    start_vec = precondition(rhs[...])
    vec_out[0] = start_vec.astype(BF16)
    send_vector(0)

    small[5].wait()
    small[6].wait()
    flux_turned[...] = flux[...].T
    trace_turned[...] = trace[...].T
    for e in range(own):
        solved[e] = nt(trace_turned[...], binv[e]).astype(BF16)

    send_meta.wait_recv()
    own_ids = lax.broadcasted_iota(jnp.int32, (own, slots), 0)
    member_ids = lax.broadcasted_iota(jnp.int32, (n_face * own, slots), 0)
    pick = (member_ids == meta_in[0:1, 0:slots]).astype(F32).T.astype(BF16)
    gather_rows = (own_ids == meta_in[1:2, 0:slots]).astype(F32)
    gather_rows = jnp.concatenate([gather_rows, gather_rows], axis=1).astype(BF16)

    def picked(blocks):
        return nn(pick, blocks.astype(F32).reshape(n_face * own, nv).astype(BF16))

    await_recv(state_in, setup_send.at[2], setup_recv.at[2], (ahead, f))
    speeds = 1.0 + 0.5 * jnp.tanh(picked(state_in[...]))
    send_metric.wait_recv()

    def operate(step, vector):
        await_recv(vec_in.at[step], vec_send.at[step], vec_recv.at[step], (ahead, f))
        lifted = nn(picked(vec_in[step]).astype(BF16), trace[...])
        spread = nn(two_terms(lifted * metric_in[...].astype(F32)), flux_turned[...])
        scaled = (spread[:slots] + spread[slots:]) * speeds
        summed = nn(gather_rows, two_terms(scaled))
        return vector + lift_and_precondition(summed)

    first_vec = operate(0, start_vec)
    vec_out[1] = first_vec.astype(BF16)
    send_vector(1)
    lane_ids = lax.broadcasted_iota(jnp.int32, (1, LANES), 1)

    def total_at(lane, x):
        column = jnp.sum(x, axis=1, keepdims=True)
        return jnp.where(lane_ids == lane, jnp.sum(column, axis=0, keepdims=True), 0.0)

    early = total_at(0, first_vec * first_vec) + total_at(3, start_vec * first_vec)
    second_vec = operate(1, first_vec)

    partial = (
        early
        + total_at(1, first_vec * second_vec)
        + total_at(2, second_vec * second_vec)
        + total_at(4, start_vec * second_vec)
    )
    base = 0
    for index, peers in enumerate(stages):
        sums_out[index] = partial
        for j, peer in enumerate(peers):
            pltpu.make_async_remote_copy(
                sums_out.at[index],
                sums_in.at[base + j],
                sums_send.at[index],
                sums_recv.at[index],
                peer,
                MESH,
            ).start()
        landed = sums_in.at[pl.ds(base, len(peers))]
        await_recv(landed, sums_send.at[index], sums_recv.at[index], (ahead, f))
        partial += jnp.sum(sums_in[base : base + len(peers)], axis=0)
        base += len(peers)

    norm_first = partial[:, 0:1]
    cross_term = partial[:, 1:2]
    norm_second = partial[:, 2:3]
    proj_first = partial[:, 3:4]
    proj_second = partial[:, 4:5]
    ridge = 0.001 * (norm_first + norm_second)
    determinant = (norm_first + ridge) * (norm_second + ridge) - cross_term * cross_term
    coef_first = (proj_first * (norm_second + ridge) - proj_second * cross_term) / determinant
    coef_second = (proj_second * (norm_first + ridge) - proj_first * cross_term) / determinant
    terms_ref[0] = coef_first * start_vec
    terms_ref[1] = coef_second * first_vec
    terms_ref[2] = start_vec - coef_first * first_vec
    terms_ref[3] = coef_second * second_vec

    send_meta.wait_send()
    send_metric.wait_send()
    await_send(state_in, setup_send.at[2], setup_recv.at[2], (ahead, f))
    for step in range(2):
        await_send(vec_in.at[step], vec_send.at[step], vec_recv.at[step], (ahead, f))
    base = 0
    for index, peers in enumerate(stages):
        landed = sums_in.at[pl.ds(base, len(peers))]
        await_send(landed, sums_send.at[index], sums_recv.at[index], (ahead, f))
        base += len(peers)


def on_device(
    n_dom,
    n_face,
    elem_state,
    face_metric,
    right_side,
    block_inverse,
    trace_basis,
    flux_basis,
    face_rows,
    face_cols,
    face_counts,
):
    own, nv = right_side.shape
    slots = face_rows.shape[0]
    radices = radices_of(n_dom)
    exchanges = n_face * radices[0] - 1 + sum(r - 1 for r in radices[1:])
    dma = pltpu.SemaphoreType.DMA
    vmem = pl.BlockSpec(memory_space=pltpu.VMEM)
    hbm = pl.BlockSpec(memory_space=pltpu.HBM)
    terms = pl.pallas_call(
        functools.partial(kernel, n_dom, n_face),
        out_shape=pltpu.VMEM((4, own, nv), F32),
        in_specs=[hbm] * 9,
        out_specs=vmem,
        scratch_shapes=[
            pltpu.VMEM((own, nv), BF16),
            pltpu.VMEM((own, nv), F32),
            pltpu.VMEM((own, nv, nv), BF16),
            pltpu.VMEM((own, nv, nv), BF16),
            pltpu.VMEM((nv, nv), BF16),
            pltpu.VMEM((nv, nv), BF16),
            pltpu.VMEM((nv, nv), BF16),
            pltpu.VMEM((nv, nv), BF16),
            pltpu.VMEM((1, slots), jnp.int32),
            pltpu.VMEM((1, slots), jnp.int32),
            pltpu.VMEM((1, 1), jnp.int32),
            pltpu.VMEM((n_face, own, nv), BF16),
            pltpu.VMEM((8, LANES), jnp.int32),
            pltpu.VMEM((8, LANES), jnp.int32),
            pltpu.VMEM((slots, nv), BF16),
            pltpu.VMEM((2, own, nv), BF16),
            pltpu.VMEM((2, n_face, own, nv), BF16),
            pltpu.VMEM((len(radices), 1, LANES), F32),
            pltpu.VMEM((exchanges, 1, LANES), F32),
            dma((own + 7,)),
            dma((3,)),
            dma((3,)),
            dma((2,)),
            dma((2,)),
            dma((len(radices),)),
            dma((len(radices),)),
        ],
        compiler_params=pltpu.CompilerParams(
            collective_id=0, has_side_effects=True, vmem_limit_bytes=24 * 1024 * 1024
        ),
    )(
        *(
            pltpu.with_memory_space_constraint(operand, pltpu.HBM)
            for operand in (
                elem_state,
                face_metric,
                right_side,
                block_inverse,
                trace_basis,
                flux_basis,
                face_rows.reshape(1, slots),
                face_cols.reshape(1, slots),
            )
        ),
        face_counts.reshape(1, 1),
    )
    return terms[0] + terms[1], terms[2] - terms[3]


def solution(mesh):
    split = P(("dom", "face"))
    return jax.shard_map(
        functools.partial(on_device, mesh.shape["dom"], mesh.shape["face"]),
        mesh=mesh,
        in_specs=(
            P(("dom", "face"), None),
            P(("dom", "face"), None),
            P(("dom", "face"), None),
            P(("dom", "face"), None, None),
            P(),
            P(),
            split,
            split,
            split,
        ),
        out_specs=(P(("dom", "face"), None), P(("dom", "face"), None)),
        check_vma=False,
    )
```

```python
import functools

import jax
import jax.numpy as jnp
from jax import lax
from jax.experimental import pallas as pl
from jax.experimental.pallas import tpu as pltpu
from jax.sharding import PartitionSpec as P

MESH = pl.DeviceIdType.MESH
F32 = jnp.float32
BF16 = jnp.bfloat16
LANES = 128
MAX_RADIX = 8


def radices_of(count):
    radices = []
    while count > 1:
        best = next((r for r in range(MAX_RADIX, 1, -1) if count % r == 0), None)
        if best is None:
            best = next(r for r in range(MAX_RADIX + 1, count + 1) if count % r == 0)
        radices.append(best)
        count //= best
    return radices


def nn(a, b):
    return jnp.dot(a, b, preferred_element_type=F32)


def nt(a, b):
    return lax.dot_general(a, b, (((1,), (1,)), ((), ())), preferred_element_type=F32)


def two_terms(x):
    high = x.astype(BF16).astype(F32)
    return jnp.concatenate([high, x - high], axis=0).astype(BF16)


def await_recv(ref, send_sem, recv_sem, peer):
    pltpu.make_async_remote_copy(ref, ref, send_sem, recv_sem, peer, MESH).wait_recv()


def await_send(ref, send_sem, recv_sem, peer):
    pltpu.make_async_remote_copy(ref, ref, send_sem, recv_sem, peer, MESH).wait_send()


def kernel(
    n_dom,
    n_face,
    state_hbm,
    metric_hbm,
    rhs_hbm,
    binv_hbm,
    trace_hbm,
    flux_hbm,
    rows_hbm,
    cols_hbm,
    count_hbm,
    terms_ref,
    state,
    rhs,
    binv,
    solved,
    trace,
    trace_turned,
    flux,
    flux_turned,
    rows,
    cols,
    count,
    state_in,
    meta_out,
    meta_in,
    metric_in,
    vec_out,
    vec_in,
    sums_out,
    sums_in,
    load_sem,
    setup_send,
    setup_recv,
    vec_send,
    vec_recv,
    sums_send,
    sums_recv,
):
    d = lax.axis_index("dom")
    f = lax.axis_index("face")
    ahead = lax.rem(d + 1, n_dom)
    behind = lax.rem(d + n_dom - 1, n_dom)
    own, nv = rhs.shape
    slots = metric_in.shape[0]

    small = [
        pltpu.make_async_copy(src, dst, load_sem.at[own + at])
        for at, (src, dst) in enumerate(
            (
                (rhs_hbm, rhs),
                (cols_hbm, cols),
                (rows_hbm, rows),
                (count_hbm, count),
                (state_hbm, state),
                (trace_hbm, trace),
                (flux_hbm, flux),
            )
        )
    ]
    loads = [
        pltpu.make_async_copy(binv_hbm.at[e], binv.at[e], load_sem.at[e]) for e in range(own)
    ]
    for load in small[:5] + loads + small[5:]:
        load.start()

    radices = radices_of(n_dom)
    low = lax.rem(d, radices[0])
    group = n_face * radices[0]
    flat = low * n_face + f
    stages = []
    peers = []
    for j in range(group - 1, 0, -1):
        other = lax.rem(flat + j, group)
        peers.append((d - low + other // n_face, lax.rem(other, n_face)))
    stages.append(peers)
    stride = radices[0]
    for radix in radices[1:]:
        digit = lax.rem(d // stride, radix)
        stages.append(
            [(d + (lax.rem(digit + j, radix) - digit) * stride, f) for j in range(1, radix)]
        )
        stride *= radix

    barrier = pltpu.get_barrier_semaphore()
    greeted = 0
    greet = [peer for peers in stages for peer in peers]
    if len(radices) > 1:
        greet += [(dom, peer) for peer in range(n_face) for dom in (ahead, behind)]
    for peer in greet:
        pl.semaphore_signal(barrier, inc=1, device_id=peer, device_id_type=MESH)
        greeted += 1

    row_ids = lax.broadcasted_iota(jnp.int32, (own, nv), 0)

    wide = solved.shape[1] // own

    def precondition(vector):
        rounded = vector.astype(BF16)
        total = jnp.zeros((own, nv), F32)
        half = own // 2
        for first in range(0, own, half):
            for load in loads[first : first + half]:
                load.wait()
            every = nt(rounded, binv[first : first + half].reshape(half * nv, nv))
            for e in range(half):
                block = every[:, e * nv : (e + 1) * nv]
                total += jnp.where(row_ids == first + e, block, 0.0)
        return total

    def lift_and_precondition(vector):
        both = nn(two_terms(vector), solved[...])
        every = both[:own] + both[own:]
        total = jnp.zeros((own, nv), F32)
        for e in range(own):
            block = every[:, e * wide : e * wide + nv]
            total += jnp.where(row_ids == e, block, 0.0)
        return total

    def send_vector(step):
        for peer in range(n_face):
            pltpu.make_async_remote_copy(
                vec_out.at[step],
                vec_in.at[step, f],
                vec_send.at[step],
                vec_recv.at[step],
                (ahead, peer),
                MESH,
            ).start()

    small[1].wait()
    small[2].wait()
    small[3].wait()
    small[4].wait()
    slot_ids = lax.broadcasted_iota(jnp.int32, (1, slots), 1)
    meta_out[...] = jnp.zeros_like(meta_out)
    meta_out[0:1, 0:slots] = jnp.where(slot_ids < count[...], cols[...], -1)
    meta_out[1:2, 0:slots] = rows[...]

    pl.semaphore_wait(barrier, greeted)

    send_meta = pltpu.make_async_remote_copy(
        meta_out, meta_in, setup_send.at[0], setup_recv.at[0], (ahead, f), MESH
    )
    send_meta.start()
    for peer in range(n_face):
        pltpu.make_async_remote_copy(
            state, state_in.at[f], setup_send.at[2], setup_recv.at[2], (ahead, peer), MESH
        ).start()
    send_metric = pltpu.make_async_remote_copy(
        metric_hbm, metric_in, setup_send.at[1], setup_recv.at[1], (ahead, f), MESH
    )
    send_metric.start()

    small[0].wait()
    start_vec = precondition(rhs[...])
    vec_out[0] = start_vec.astype(BF16)
    send_vector(0)

    small[5].wait()
    small[6].wait()
    flux_turned[...] = flux[...].T
    trace_turned[...] = trace[...].T
    for e in range(own):
        block = nt(trace_turned[...], binv[e])
        block = jnp.concatenate([block, jnp.zeros((nv, wide - nv), F32)], axis=1)
        solved[:, e * wide : (e + 1) * wide] = block.astype(BF16)

    send_meta.wait_recv()
    own_ids = lax.broadcasted_iota(jnp.int32, (own, slots), 0)
    member_ids = lax.broadcasted_iota(jnp.int32, (n_face * own, slots), 0)
    pick = (member_ids == meta_in[0:1, 0:slots]).astype(F32).T.astype(BF16)
    gather_rows = (own_ids == meta_in[1:2, 0:slots]).astype(F32)
    gather_rows = jnp.concatenate([gather_rows, gather_rows], axis=1).astype(BF16)

    def picked(blocks):
        return nn(pick, blocks.astype(F32).reshape(n_face * own, nv).astype(BF16))

    await_recv(state_in, setup_send.at[2], setup_recv.at[2], (ahead, f))
    speeds = 1.0 + 0.5 * jnp.tanh(picked(state_in[...]))
    send_metric.wait_recv()

    def operate(step, vector):
        await_recv(vec_in.at[step], vec_send.at[step], vec_recv.at[step], (ahead, f))
        lifted = nn(picked(vec_in[step]).astype(BF16), trace[...])
        spread = nn(two_terms(lifted * metric_in[...].astype(F32)), flux_turned[...])
        scaled = (spread[:slots] + spread[slots:]) * speeds
        summed = nn(gather_rows, two_terms(scaled))
        return vector + lift_and_precondition(summed)

    first_vec = operate(0, start_vec)
    vec_out[1] = first_vec.astype(BF16)
    send_vector(1)
    lane_ids = lax.broadcasted_iota(jnp.int32, (1, LANES), 1)

    def total_at(lane, x):
        column = jnp.sum(x, axis=1, keepdims=True)
        return jnp.where(lane_ids == lane, jnp.sum(column, axis=0, keepdims=True), 0.0)

    early = total_at(0, first_vec * first_vec) + total_at(3, start_vec * first_vec)
    second_vec = operate(1, first_vec)

    partial = (
        early
        + total_at(1, first_vec * second_vec)
        + total_at(2, second_vec * second_vec)
        + total_at(4, start_vec * second_vec)
    )
    base = 0
    for index, peers in enumerate(stages):
        sums_out[index] = partial
        for j, peer in enumerate(peers):
            pltpu.make_async_remote_copy(
                sums_out.at[index],
                sums_in.at[base + j],
                sums_send.at[index],
                sums_recv.at[index],
                peer,
                MESH,
            ).start()
        landed = sums_in.at[pl.ds(base, len(peers))]
        await_recv(landed, sums_send.at[index], sums_recv.at[index], (ahead, f))
        partial += jnp.sum(sums_in[base : base + len(peers)], axis=0)
        base += len(peers)

    norm_first = partial[:, 0:1]
    cross_term = partial[:, 1:2]
    norm_second = partial[:, 2:3]
    proj_first = partial[:, 3:4]
    proj_second = partial[:, 4:5]
    ridge = 0.001 * (norm_first + norm_second)
    determinant = (norm_first + ridge) * (norm_second + ridge) - cross_term * cross_term
    coef_first = (proj_first * (norm_second + ridge) - proj_second * cross_term) / determinant
    coef_second = (proj_second * (norm_first + ridge) - proj_first * cross_term) / determinant
    terms_ref[0] = coef_first * start_vec
    terms_ref[1] = coef_second * first_vec
    terms_ref[2] = start_vec - coef_first * first_vec
    terms_ref[3] = coef_second * second_vec

    send_meta.wait_send()
    send_metric.wait_send()
    await_send(state_in, setup_send.at[2], setup_recv.at[2], (ahead, f))
    for step in range(2):
        await_send(vec_in.at[step], vec_send.at[step], vec_recv.at[step], (ahead, f))
    base = 0
    for index, peers in enumerate(stages):
        landed = sums_in.at[pl.ds(base, len(peers))]
        await_send(landed, sums_send.at[index], sums_recv.at[index], (ahead, f))
        base += len(peers)


def on_device(
    n_dom,
    n_face,
    elem_state,
    face_metric,
    right_side,
    block_inverse,
    trace_basis,
    flux_basis,
    face_rows,
    face_cols,
    face_counts,
):
    own, nv = right_side.shape
    slots = face_rows.shape[0]
    radices = radices_of(n_dom)
    exchanges = n_face * radices[0] - 1 + sum(r - 1 for r in radices[1:])
    dma = pltpu.SemaphoreType.DMA
    vmem = pl.BlockSpec(memory_space=pltpu.VMEM)
    hbm = pl.BlockSpec(memory_space=pltpu.HBM)
    terms = pl.pallas_call(
        functools.partial(kernel, n_dom, n_face),
        out_shape=pltpu.VMEM((4, own, nv), F32),
        in_specs=[hbm] * 9,
        out_specs=vmem,
        scratch_shapes=[
            pltpu.VMEM((own, nv), BF16),
            pltpu.VMEM((own, nv), F32),
            pltpu.VMEM((own, nv, nv), BF16),
            pltpu.VMEM((nv, own * -(-nv // LANES) * LANES), BF16),
            pltpu.VMEM((nv, nv), BF16),
            pltpu.VMEM((nv, nv), BF16),
            pltpu.VMEM((nv, nv), BF16),
            pltpu.VMEM((nv, nv), BF16),
            pltpu.VMEM((1, slots), jnp.int32),
            pltpu.VMEM((1, slots), jnp.int32),
            pltpu.VMEM((1, 1), jnp.int32),
            pltpu.VMEM((n_face, own, nv), BF16),
            pltpu.VMEM((8, LANES), jnp.int32),
            pltpu.VMEM((8, LANES), jnp.int32),
            pltpu.VMEM((slots, nv), BF16),
            pltpu.VMEM((2, own, nv), BF16),
            pltpu.VMEM((2, n_face, own, nv), BF16),
            pltpu.VMEM((len(radices), 1, LANES), F32),
            pltpu.VMEM((exchanges, 1, LANES), F32),
            dma((own + 7,)),
            dma((3,)),
            dma((3,)),
            dma((2,)),
            dma((2,)),
            dma((len(radices),)),
            dma((len(radices),)),
        ],
        compiler_params=pltpu.CompilerParams(
            collective_id=0, has_side_effects=True, vmem_limit_bytes=24 * 1024 * 1024
        ),
    )(
        *(
            pltpu.with_memory_space_constraint(operand, pltpu.HBM)
            for operand in (
                elem_state,
                face_metric,
                right_side,
                block_inverse,
                trace_basis,
                flux_basis,
                face_rows.reshape(1, slots),
                face_cols.reshape(1, slots),
            )
        ),
        face_counts.reshape(1, 1),
    )
    return terms[0] + terms[1], terms[2] - terms[3]


def solution(mesh):
    split = P(("dom", "face"))
    return jax.shard_map(
        functools.partial(on_device, mesh.shape["dom"], mesh.shape["face"]),
        mesh=mesh,
        in_specs=(
            P(("dom", "face"), None),
            P(("dom", "face"), None),
            P(("dom", "face"), None),
            P(("dom", "face"), None, None),
            P(),
            P(),
            split,
            split,
            split,
        ),
        out_specs=(P(("dom", "face"), None), P(("dom", "face"), None)),
        check_vma=False,
    )
```

```python
import functools

import jax
import jax.numpy as jnp
from jax import lax
from jax.experimental import pallas as pl
from jax.experimental.pallas import tpu as pltpu
from jax.sharding import PartitionSpec as P

MESH = pl.DeviceIdType.MESH
F32 = jnp.float32
BF16 = jnp.bfloat16
LANES = 128
MAX_RADIX = 8


def radices_of(count):
    radices = []
    while count > 1:
        best = next((r for r in range(MAX_RADIX, 1, -1) if count % r == 0), None)
        if best is None:
            best = next(r for r in range(MAX_RADIX + 1, count + 1) if count % r == 0)
        radices.append(best)
        count //= best
    return radices


def nn(a, b):
    return jnp.dot(a, b, preferred_element_type=F32)


def nt(a, b):
    return lax.dot_general(a, b, (((1,), (1,)), ((), ())), preferred_element_type=F32)


def two_terms(x):
    high = x.astype(BF16).astype(F32)
    return jnp.concatenate([high, x - high], axis=0).astype(BF16)


def await_recv(ref, send_sem, recv_sem, peer):
    pltpu.make_async_remote_copy(ref, ref, send_sem, recv_sem, peer, MESH).wait_recv()


def await_send(ref, send_sem, recv_sem, peer):
    pltpu.make_async_remote_copy(ref, ref, send_sem, recv_sem, peer, MESH).wait_send()


def kernel(
    n_dom,
    n_face,
    state_hbm,
    metric_hbm,
    rhs_hbm,
    binv_hbm,
    trace_hbm,
    flux_hbm,
    rows_hbm,
    cols_hbm,
    count_hbm,
    terms_ref,
    state,
    rhs,
    binv,
    solved,
    trace,
    trace_turned,
    flux,
    flux_turned,
    rows,
    cols,
    count,
    state_in,
    meta_out,
    meta_in,
    metric_in,
    vec_out,
    vec_in,
    sums_out,
    sums_in,
    load_sem,
    setup_send,
    setup_recv,
    vec_send,
    vec_recv,
    sums_send,
    sums_recv,
):
    d = lax.axis_index("dom")
    f = lax.axis_index("face")
    ahead = lax.rem(d + 1, n_dom)
    behind = lax.rem(d + n_dom - 1, n_dom)
    own, nv = rhs.shape
    slots = metric_in.shape[0]

    small = [
        pltpu.make_async_copy(src, dst, load_sem.at[own + at])
        for at, (src, dst) in enumerate(
            (
                (rhs_hbm, rhs),
                (cols_hbm, cols),
                (rows_hbm, rows),
                (count_hbm, count),
                (state_hbm, state),
                (trace_hbm, trace),
                (flux_hbm, flux),
            )
        )
    ]
    loads = [
        pltpu.make_async_copy(binv_hbm.at[e], binv.at[e], load_sem.at[e]) for e in range(own)
    ]
    for load in small[:5] + loads + small[5:]:
        load.start()

    radices = radices_of(n_dom)
    low = lax.rem(d, radices[0])
    group = n_face * radices[0]
    flat = low * n_face + f
    stages = []
    peers = []
    for j in range(group - 1, 0, -1):
        other = lax.rem(flat + j, group)
        peers.append((d - low + other // n_face, lax.rem(other, n_face)))
    stages.append(peers)
    stride = radices[0]
    for radix in radices[1:]:
        digit = lax.rem(d // stride, radix)
        stages.append(
            [(d + (lax.rem(digit + j, radix) - digit) * stride, f) for j in range(1, radix)]
        )
        stride *= radix

    barrier = pltpu.get_barrier_semaphore()
    greeted = 0
    greet = [peer for peers in stages for peer in peers]
    if len(radices) > 1:
        greet += [(dom, peer) for peer in range(n_face) for dom in (ahead, behind)]
    for peer in greet:
        pl.semaphore_signal(barrier, inc=1, device_id=peer, device_id_type=MESH)
        greeted += 1

    row_ids = lax.broadcasted_iota(jnp.int32, (own, nv), 0)

    wide = solved.shape[1] // own

    def precondition(vector):
        rounded = vector.astype(BF16)
        total = jnp.zeros((own, nv), F32)
        half = own // 2
        for first in range(0, own, half):
            for load in loads[first : first + half]:
                load.wait()
            every = nt(rounded, binv[first : first + half].reshape(half * nv, nv))
            for e in range(half):
                block = every[:, e * nv : (e + 1) * nv]
                total += jnp.where(row_ids == first + e, block, 0.0)
        return total

    def lift_and_precondition(vector):
        both = nn(two_terms(vector), solved[...])
        every = both[:own] + both[own:]
        total = jnp.zeros((own, nv), F32)
        for e in range(own):
            block = every[:, e * wide : e * wide + nv]
            total += jnp.where(row_ids == e, block, 0.0)
        return total

    def send_vector(step):
        for peer in range(n_face):
            pltpu.make_async_remote_copy(
                vec_out.at[step],
                vec_in.at[step, f],
                vec_send.at[step],
                vec_recv.at[step],
                (ahead, peer),
                MESH,
            ).start()

    small[1].wait()
    small[2].wait()
    small[3].wait()
    small[4].wait()
    slot_ids = lax.broadcasted_iota(jnp.int32, (1, slots), 1)
    meta_out[...] = jnp.zeros_like(meta_out)
    meta_out[0:1, 0:slots] = jnp.where(slot_ids < count[...], cols[...], -1)
    meta_out[1:2, 0:slots] = rows[...]

    pl.semaphore_wait(barrier, greeted)

    send_meta = pltpu.make_async_remote_copy(
        meta_out, meta_in, setup_send.at[0], setup_recv.at[0], (ahead, f), MESH
    )
    send_meta.start()
    for peer in range(n_face):
        pltpu.make_async_remote_copy(
            state, state_in.at[f], setup_send.at[2], setup_recv.at[2], (ahead, peer), MESH
        ).start()
    send_metric = pltpu.make_async_remote_copy(
        metric_hbm, metric_in, setup_send.at[1], setup_recv.at[1], (ahead, f), MESH
    )
    send_metric.start()

    small[0].wait()
    start_vec = precondition(rhs[...])
    vec_out[0] = start_vec.astype(BF16)
    send_vector(0)

    small[5].wait()
    small[6].wait()
    flux_turned[...] = flux[...].T
    trace_turned[...] = trace[...].T
    for e in range(own):
        block = nt(trace_turned[...], binv[e])
        block = jnp.concatenate([block, jnp.zeros((nv, wide - nv), F32)], axis=1)
        solved[:, e * wide : (e + 1) * wide] = block.astype(BF16)

    send_meta.wait_recv()
    own_ids = lax.broadcasted_iota(jnp.int32, (own, slots), 0)
    member_ids = lax.broadcasted_iota(jnp.int32, (n_face * own, slots), 0)
    pick = (member_ids == meta_in[0:1, 0:slots]).astype(F32).T.astype(BF16)
    gather_rows = (own_ids == meta_in[1:2, 0:slots]).astype(F32).astype(BF16)

    def picked(blocks):
        return nn(pick, blocks.astype(F32).reshape(n_face * own, nv).astype(BF16))

    await_recv(state_in, setup_send.at[2], setup_recv.at[2], (ahead, f))
    speeds = 1.0 + 0.5 * jnp.tanh(picked(state_in[...]))
    send_metric.wait_recv()

    def operate(step, vector):
        await_recv(vec_in.at[step], vec_send.at[step], vec_recv.at[step], (ahead, f))
        lifted = nn(picked(vec_in[step]).astype(BF16), trace[...])
        spread = nn((lifted * metric_in[...].astype(F32)).astype(BF16), flux_turned[...])
        summed = nn(gather_rows, (spread * speeds).astype(BF16))
        return vector + lift_and_precondition(summed)

    first_vec = operate(0, start_vec)
    vec_out[1] = first_vec.astype(BF16)
    send_vector(1)
    lane_ids = lax.broadcasted_iota(jnp.int32, (1, LANES), 1)

    def total_at(lane, x):
        column = jnp.sum(x, axis=1, keepdims=True)
        return jnp.where(lane_ids == lane, jnp.sum(column, axis=0, keepdims=True), 0.0)

    early = total_at(0, first_vec * first_vec) + total_at(3, start_vec * first_vec)
    second_vec = operate(1, first_vec)

    partial = (
        early
        + total_at(1, first_vec * second_vec)
        + total_at(2, second_vec * second_vec)
        + total_at(4, start_vec * second_vec)
    )
    base = 0
    for index, peers in enumerate(stages):
        sums_out[index] = partial
        for j, peer in enumerate(peers):
            pltpu.make_async_remote_copy(
                sums_out.at[index],
                sums_in.at[base + j],
                sums_send.at[index],
                sums_recv.at[index],
                peer,
                MESH,
            ).start()
        landed = sums_in.at[pl.ds(base, len(peers))]
        await_recv(landed, sums_send.at[index], sums_recv.at[index], (ahead, f))
        partial += jnp.sum(sums_in[base : base + len(peers)], axis=0)
        base += len(peers)

    norm_first = partial[:, 0:1]
    cross_term = partial[:, 1:2]
    norm_second = partial[:, 2:3]
    proj_first = partial[:, 3:4]
    proj_second = partial[:, 4:5]
    ridge = 0.001 * (norm_first + norm_second)
    determinant = (norm_first + ridge) * (norm_second + ridge) - cross_term * cross_term
    coef_first = (proj_first * (norm_second + ridge) - proj_second * cross_term) / determinant
    coef_second = (proj_second * (norm_first + ridge) - proj_first * cross_term) / determinant
    terms_ref[0] = coef_first * start_vec
    terms_ref[1] = coef_second * first_vec
    terms_ref[2] = start_vec - coef_first * first_vec
    terms_ref[3] = coef_second * second_vec

    send_meta.wait_send()
    send_metric.wait_send()
    await_send(state_in, setup_send.at[2], setup_recv.at[2], (ahead, f))
    for step in range(2):
        await_send(vec_in.at[step], vec_send.at[step], vec_recv.at[step], (ahead, f))
    base = 0
    for index, peers in enumerate(stages):
        landed = sums_in.at[pl.ds(base, len(peers))]
        await_send(landed, sums_send.at[index], sums_recv.at[index], (ahead, f))
        base += len(peers)


def on_device(
    n_dom,
    n_face,
    elem_state,
    face_metric,
    right_side,
    block_inverse,
    trace_basis,
    flux_basis,
    face_rows,
    face_cols,
    face_counts,
):
    own, nv = right_side.shape
    slots = face_rows.shape[0]
    radices = radices_of(n_dom)
    exchanges = n_face * radices[0] - 1 + sum(r - 1 for r in radices[1:])
    dma = pltpu.SemaphoreType.DMA
    vmem = pl.BlockSpec(memory_space=pltpu.VMEM)
    hbm = pl.BlockSpec(memory_space=pltpu.HBM)
    terms = pl.pallas_call(
        functools.partial(kernel, n_dom, n_face),
        out_shape=pltpu.VMEM((4, own, nv), F32),
        in_specs=[hbm] * 9,
        out_specs=vmem,
        scratch_shapes=[
            pltpu.VMEM((own, nv), BF16),
            pltpu.VMEM((own, nv), F32),
            pltpu.VMEM((own, nv, nv), BF16),
            pltpu.VMEM((nv, own * -(-nv // LANES) * LANES), BF16),
            pltpu.VMEM((nv, nv), BF16),
            pltpu.VMEM((nv, nv), BF16),
            pltpu.VMEM((nv, nv), BF16),
            pltpu.VMEM((nv, nv), BF16),
            pltpu.VMEM((1, slots), jnp.int32),
            pltpu.VMEM((1, slots), jnp.int32),
            pltpu.VMEM((1, 1), jnp.int32),
            pltpu.VMEM((n_face, own, nv), BF16),
            pltpu.VMEM((8, LANES), jnp.int32),
            pltpu.VMEM((8, LANES), jnp.int32),
            pltpu.VMEM((slots, nv), BF16),
            pltpu.VMEM((2, own, nv), BF16),
            pltpu.VMEM((2, n_face, own, nv), BF16),
            pltpu.VMEM((len(radices), 1, LANES), F32),
            pltpu.VMEM((exchanges, 1, LANES), F32),
            dma((own + 7,)),
            dma((3,)),
            dma((3,)),
            dma((2,)),
            dma((2,)),
            dma((len(radices),)),
            dma((len(radices),)),
        ],
        compiler_params=pltpu.CompilerParams(
            collective_id=0, has_side_effects=True, vmem_limit_bytes=24 * 1024 * 1024
        ),
    )(
        *(
            pltpu.with_memory_space_constraint(operand, pltpu.HBM)
            for operand in (
                elem_state,
                face_metric,
                right_side,
                block_inverse,
                trace_basis,
                flux_basis,
                face_rows.reshape(1, slots),
                face_cols.reshape(1, slots),
            )
        ),
        face_counts.reshape(1, 1),
    )
    return terms[0] + terms[1], terms[2] - terms[3]


def solution(mesh):
    split = P(("dom", "face"))
    return jax.shard_map(
        functools.partial(on_device, mesh.shape["dom"], mesh.shape["face"]),
        mesh=mesh,
        in_specs=(
            P(("dom", "face"), None),
            P(("dom", "face"), None),
            P(("dom", "face"), None),
            P(("dom", "face"), None, None),
            P(),
            P(),
            split,
            split,
            split,
        ),
        out_specs=(P(("dom", "face"), None), P(("dom", "face"), None)),
        check_vma=False,
    )
```
